256 devices in a mesh: leaf: 8 (over z_hi, x), row: 4 (over y), col: 8 (over z_lo, core).
Axes of the slice: x: 4, y: 4, z: 8 (z_hi: 2, z_lo: 4; z = z_hi * 4 + z_lo), core: 2. Of those that a mesh axis runs over, the one named last changes fastest.
Arguments:
- sigma_root: float32 [8192, 8192], P('leaf', ('row', 'col')), as said below
- structure: int32 [16, 1024], replicated, may hold values from 0 to 8191, as said below
- inv_diag: float32 [16, 2048, 2048], P('leaf', 'row', 'col'), as said below
- panel: float32 [16, 1024, 2048], P('leaf', None, 'row'), may hold values from -0.1875 to 0.1875
Outputs:
- sigma_panel: float32 [16, 1024, 2048], P('leaf', 'row', 'col')
- sigma_diag: float32 [16, 2048, 2048], P('leaf', 'row', 'col')
The draws below stay inside these ranges and needn't reach their ends.
Inputs may be any that keep to these rules, and one draw needn't show every extreme that they name: structure[h] is increasing, and of the root indices in each aligned block of 32, exactly 4 appear in structure[h]. sigma_root is symmetric. inv_diag[h] is lower triangular with a positive diagonal.
All inputs are finite; a program needn't handle non-finite values.
Results may differ from the reference program's by a relative error of at most 0.0003.
Values sent between devices are 32-bit elements; how exact they have to be, the bound alone decides.
A program may use at most 128 MiB of HBM per device.

```python
import math
import jax
import jax.numpy as jnp
from jax import lax

NR = 8192
NS = 1024
NC = 2048
CHILDREN = 16
FINE = 32
PICK = 4


def draw_sigma_root(key, part):
    key = jax.random.fold_in(key, 11)
    key_off, key_diag = jax.random.split(key, 2)
    raw = jax.random.normal(key_off, (NR, NR), jnp.float32)
    off_part = (raw + raw.T) * (2.0 / math.sqrt(2.0 * NR))
    diagonal = jnp.exp(jax.random.uniform(key_diag, (NR,), jnp.float32, math.log(1.5), math.log(3.0)))
    rows_idx = lax_iota_rows(NR)
    cols_idx = rows_idx.T
    return jnp.where(rows_idx == cols_idx, diagonal[:, None] * jnp.ones((1, NR), jnp.float32), off_part)


def lax_iota_rows(count):
    return jnp.arange(count, dtype=jnp.int32)[:, None] * jnp.ones((1, count), jnp.int32)


def draw_structure(key, part):
    key = jax.random.fold_in(key, 23)
    blocks = NR // FINE
    scores = jax.random.randint(key, (CHILDREN, blocks, FINE), 0, 65536, jnp.int32) * FINE + jnp.arange(FINE, dtype=jnp.int32)
    order = jnp.argsort(scores, axis=-1).astype(jnp.int32)
    chosen = jnp.sort(order[:, :, :PICK], axis=-1)
    index_set = chosen + (jnp.arange(blocks, dtype=jnp.int32) * FINE)[None, :, None]
    return index_set.reshape(CHILDREN, NS).astype(jnp.int32)


def draw_inv_diag(key, part):
    key = jax.random.fold_in(key, 37)
    key_low, key_diag = jax.random.split(key, 2)
    raw = jax.random.normal(key_low, (CHILDREN, NC, NC), jnp.float32)
    lower = raw * (1.5 / math.sqrt(NC))
    diagonal = jnp.exp(jax.random.uniform(key_diag, (CHILDREN, NC, 1), jnp.float32, math.log(0.7), math.log(1.4)))
    rows_idx = lax_iota_rows(NC)[None]
    cols_idx = jnp.transpose(lax_iota_rows(NC))[None]
    return jnp.where(rows_idx > cols_idx, lower, jnp.where(rows_idx == cols_idx, diagonal * jnp.ones((1, 1, NC), jnp.float32), 0.0))


def block_levels(own_key, extent, cuts, smallest, high):
    level, own = 1.0, jax.random.fold_in(own_key, 6)
    for axis_at, parts in cuts:
        draws = jnp.exp(jax.random.uniform(jax.random.fold_in(own, axis_at), (parts,), jnp.float32, smallest / len(cuts), high / len(cuts)))
        level = level * jnp.repeat(draws, extent[axis_at] // parts).reshape([-1 if axis == axis_at else 1 for axis in range(len(extent))])
    return level


def normal_values(stream_key, shape, scale, limit, pieces=(), kind=jnp.bfloat16):
    result = jax.random.normal(stream_key, shape, jnp.float32) * scale
    if len(pieces) > 0:
        result = block_levels(stream_key, shape, pieces, -0.22, 0.18) * result
    return jnp.clip(result, min=-limit, max=limit).astype(kind)


def setup_inputs(seed: int = 0) -> dict:
    splits = jax.random.split(jax.random.key(seed), 5)
    return {
        "sigma_root": draw_sigma_root(jax.random.fold_in(splits[4], 71), 0),
        "structure": draw_structure(jax.random.fold_in(splits[4], 71), 0),
        "inv_diag": draw_inv_diag(jax.random.fold_in(splits[4], 71), 0),
        "panel": normal_values(splits[3], (CHILDREN, NS, NC), NS ** -0.5, 0.1875, ((0, 8), (2, 4)), jnp.float32),
    }


def child_inverse(sigma_root, index_set, inverse_block, factor_panel):
    ancestor = jnp.take(jnp.take(sigma_root, index_set, axis=0), index_set, axis=1)
    product = jnp.dot(factor_panel, inverse_block, precision=lax.Precision.HIGHEST, preferred_element_type=jnp.float32)
    sigma_panel = -jnp.dot(ancestor, product, precision=lax.Precision.HIGHEST, preferred_element_type=jnp.float32)
    first_term = jnp.dot(inverse_block.T, inverse_block, precision=lax.Precision.HIGHEST, preferred_element_type=jnp.float32)
    second_term = jnp.dot(product.T, sigma_panel, precision=lax.Precision.HIGHEST, preferred_element_type=jnp.float32)
    return sigma_panel, first_term - second_term


def reference(sigma_root, structure, inv_diag, panel):
    def one_child(items):
        return child_inverse(sigma_root, items[0].astype(jnp.int32), items[1], items[2])

    sigma_panel, sigma_diag = lax.map(one_child, (structure, inv_diag, panel))
    return (sigma_panel, sigma_diag)
```

```python
import jax
import jax.numpy as jnp
from jax import lax
from jax.sharding import PartitionSpec as P

HIGHEST = lax.Precision.HIGHEST


def mm(spec, a, b):
    return jnp.einsum(spec, a, b, precision=HIGHEST, preferred_element_type=jnp.float32)


def body(sigma_root, structure, inv_diag, panel):
    leaf_pos = lax.axis_index("leaf")
    row_pos = lax.axis_index("row")
    col_pos = lax.axis_index("col")
    leaf_count = lax.axis_size("leaf")
    row_count = lax.axis_size("row")
    col_count = lax.axis_size("col")
    block_rows, block_cols = sigma_root.shape
    per_group = inv_diag.shape[0]
    children, struct_len = structure.shape
    row_share = struct_len // leaf_count
    col_share = struct_len // (row_count * col_count)
    grid_pos = row_pos * col_count + col_pos

    rows = lax.dynamic_slice_in_dim(structure, leaf_pos * row_share, row_share, 1) - leaf_pos * block_rows
    cols = lax.dynamic_slice_in_dim(structure, grid_pos * col_share, col_share, 1) - grid_pos * block_cols
    pick_col = (cols[:, :, None] == jnp.arange(block_cols)[None, None, :]).astype(jnp.float32)
    pick_row = (rows[:, None, :] == jnp.arange(block_rows)[None, :, None]).astype(jnp.float32)
    by_col = mm("htc,rc->htr", pick_col, sigma_root)
    picked = mm("htr,hrs->hts", by_col, pick_row)
    picked = picked.reshape(leaf_count, per_group, col_share, row_share)
    got = lax.all_to_all(picked, "leaf", 0, 0)
    own_anc = got.transpose(1, 2, 0, 3).reshape(per_group, col_share, struct_len)
    gathered = lax.all_gather(inv_diag, "col", axis=2, tiled=True)
    ancestor = lax.all_gather(own_anc, "col", axis=1, tiled=True)

    product = lax.psum(mm("msk,mkj->msj", panel, inv_diag), "row")
    sigma_panel = -mm("mts,msj->mtj", ancestor, product)
    panel_full = lax.all_gather(sigma_panel, "row", axis=1, tiled=True)
    right = inv_diag - mm("msk,msj->mkj", panel, panel_full)
    partials = mm("mkn,mkj->mnj", gathered, right)
    sigma_diag = lax.psum_scatter(partials, "row", scatter_dimension=1, tiled=True)
    return (sigma_panel, sigma_diag)


def solution(mesh):
    placed = (P("leaf", ("row", "col")), P(), P("leaf", "row", "col"), P("leaf", None, "row"))
    return jax.shard_map(
        body,
        mesh=mesh,
        in_specs=placed,
        out_specs=(P("leaf", "row", "col"), P("leaf", "row", "col")),
        check_vma=False,
    )
```

```python
from functools import partial

import jax
import jax.numpy as jnp
from jax import lax
from jax.experimental import pallas as pl
from jax.experimental.pallas import tpu as pltpu
from jax.sharding import PartitionSpec as P

MESH = pl.DeviceIdType.MESH
F32 = jnp.float32
BF16 = jnp.bfloat16


def split(x):
    high = x.astype(BF16)
    return high, (x - high.astype(F32)).astype(BF16)


def split3(x):
    high = x.astype(BF16)
    rest = x - high.astype(F32)
    mid = rest.astype(BF16)
    return high, mid, (rest - mid.astype(F32)).astype(BF16)


def dot(a, b):
    return lax.dot_general(a, b, (((1,), (0,)), ((), ())), preferred_element_type=F32)


def dot_t(a, b):
    return lax.dot_general(a, b, (((1,), (1,)), ((), ())), preferred_element_type=F32)


def dot3(a, b):
    ah, al = split(a)
    bh, bl = split(b)
    return dot(ah, bh) + (dot(ah, bl) + dot(al, bh))


def kernel(
    sizes,
    w_ref, i_ref, sig_ref, st_ref, pick_ref,
    sp_ref, sd_ref,
    ig, aa, asend, yt, pp, ph, pr, pf, qt, it, nt, dp, dh, dr,
    z_ss, z_rs, b_ss, b_rs, l_ss, l_rs, p_ss, p_rs, a_ss, a_rs, s_ss, s_rs, d_ss, d_rs,
):
    leaves, rows, cols, group, ns, kb, cb, root_rows = sizes
    depth = cols // 2
    tb = ns // rows
    ra = ns // (rows * cols)
    sa = ns // leaves
    leaf = lax.axis_index("leaf")
    y = lax.axis_index("row")
    c = lax.axis_index("col")
    z = c // 2
    core = c % 2
    y_next, y_prev, y_far = (y + 1) % rows, (y + rows - 1) % rows, (y + 2) % rows
    sibling = c + 1 - 2 * core

    def copy(src, dst, ss, rs, target):
        return pltpu.make_async_remote_copy(
            src_ref=src, dst_ref=dst, send_sem=ss, recv_sem=rs, device_id=target, device_id_type=MESH
        )

    barrier = pltpu.get_barrier_semaphore()
    for target in ({"row": y_next}, {"row": y_prev}, {"col": sibling}):
        pl.semaphore_signal(barrier, inc=1, device_id=target, device_id_type=MESH)
    for d in range(1, leaves):
        pl.semaphore_signal(barrier, inc=1, device_id={"leaf": (leaf + d) % leaves}, device_id_type=MESH)

    @pl.when(z > 0)
    def _():
        pl.semaphore_signal(barrier, inc=1, device_id={"col": c - 2}, device_id_type=MESH)

    @pl.when(z < depth - 1)
    def _():
        pl.semaphore_signal(barrier, inc=1, device_id={"col": c + 2}, device_id_type=MESH)

    def view(item, slot):
        if item < group:
            return ig.at[slot, item]
        return aa.at[:, pl.ds(pl.multiple_of(slot * ra, ra), ra), :]

    def z_copy(item, way, step):
        slot = c - 2 * (step - 1) if way == 0 else c + 2 * (step - 1)
        target = c + 2 if way == 0 else c - 2
        return copy(
            view(item, slot), view(item, slot),
            z_ss.at[item, way, step - 1], z_rs.at[item, way, step - 1], {"col": target},
        )

    def z_sends(way, step):
        if way == 0:
            return jnp.logical_and(z < depth - 1, z >= step - 1)
        return jnp.logical_and(z > 0, z + step - 1 <= depth - 1)

    def z_gets(way, step):
        return z >= step if way == 0 else z + step <= depth - 1

    def b_copy(item, origin):
        slot = 2 * origin + core
        return copy(view(item, slot), view(item, slot), b_ss.at[item, origin], b_rs.at[item, origin], {"col": sibling})

    def z_start(item, way, step):
        @pl.when(z_sends(way, step))
        def _():
            z_copy(item, way, step).start()

    def z_own(item):
        z_start(item, 0, 1)
        z_start(item, 1, 1)
        b_copy(item, z).start()

    def z_relay(item, step):
        for way in range(2):
            @pl.when(z_gets(way, step))
            def _():
                origin = z - step if way == 0 else z + step
                slot = 2 * origin + core
                copy(
                    view(item, slot), view(item, slot),
                    z_ss.at[item, way, step - 1], z_rs.at[item, way, step - 1], {"col": sibling},
                ).wait_recv()
                if step < depth - 1:
                    z_start(item, way, step + 1)
                b_copy(item, origin).start()

    def z_last(item):
        for origin in range(depth):
            slot = 2 * origin + 1 - core
            copy(
                view(item, slot), view(item, slot), b_ss.at[item, origin], b_rs.at[item, origin], {"col": sibling}
            ).wait_recv()

    def z_sent(item):
        for way in range(2):
            for step in range(1, depth):
                @pl.when(z_sends(way, step))
                def _():
                    z_copy(item, way, step).wait_send()
        for origin in range(depth):
            b_copy(item, origin).wait_send()

    def rs_copies(part, half, whole, ss, rs):
        right, left = {"row": y_next}, {"row": y_prev}
        plan = (
            (part(y_far, 0), half(0), right),
            (part(y_far, 1), half(1), left),
            (part(y_next, 1), whole(0, 1), right),
            (part(y_prev, 0), whole(1, 0), left),
            (part(y_next, 0), whole(0, 0), right),
            (part(y_prev, 1), whole(1, 1), left),
        )
        return [copy(src, dst, ss.at[k], rs.at[k], target) for k, (src, dst, target) in enumerate(plan)]

    def p_part(h):
        return lambda s, k: pp.at[h, pl.ds(pl.multiple_of(s * tb + k * (tb // 2), tb // 2), tb // 2), :]

    def p_rs_copies(h):
        return rs_copies(
            p_part(h), lambda k: ph.at[h, k],
            lambda w, k: pr.at[h, w, k], p_ss.at[h], p_rs.at[h],
        )

    def d_part(h):
        return lambda s, k: dp.at[h, 2 * s + k]

    def d_rs_copies(h):
        return rs_copies(
            d_part(h), lambda k: dh.at[h, k],
            lambda w, k: dr.at[h, w, k], d_ss.at[h], d_rs.at[h],
        )

    def rs_round1(copies):
        for k in range(4):
            copies[k].start()

    def rs_round2(copies, part, half):
        copies[0].wait_recv()
        mine = part(y_next, 0)
        mine[...] = mine[...] + half(0)[...]
        copies[4].start()
        copies[1].wait_recv()
        mine = part(y_prev, 1)
        mine[...] = mine[...] + half(1)[...]
        copies[5].start()

    def rs_arrived(copies):
        for k in range(2, 6):
            copies[k].wait_recv()

    def sent(copies):
        for one in copies:
            one.wait_send()

    def ag_copies(slot, ss, rs):
        right, left = {"row": y_next}, {"row": y_prev}
        plan = (
            (slot(y, 0), right), (slot(y, 1), left), (slot(y, 1), right), (slot(y, 0), left),
            (slot(y_prev, 0), right), (slot(y_next, 1), left),
        )
        return [copy(src, src, ss.at[k], rs.at[k], target) for k, (src, target) in enumerate(plan)]

    def pf_copies(h):
        slot = lambda s, k: pf.at[h, pl.ds(pl.multiple_of(s * tb + k * (tb // 2), tb // 2), tb // 2), :]
        return ag_copies(slot, a_ss.at[h], a_rs.at[h])

    def qt_copies(h):
        slot = lambda s, k: qt.at[h, s, pl.ds(k * (cb // 2), cb // 2), :]
        return ag_copies(slot, s_ss.at[h], s_rs.at[h])

    def ag_round1(copies):
        for k in range(4):
            copies[k].start()

    def ag_round2(copies):
        copies[0].wait_recv()
        copies[4].start()
        copies[1].wait_recv()
        copies[5].start()

    def ag_arrived(copies):
        for k in range(2, 6):
            copies[k].wait_recv()

    def product_partial(h):
        @pl.loop(0, rows)
        def _(s):
            at = pl.ds(pl.multiple_of(s * tb, tb), tb)
            pp[h, at, :] = dot3(w_ref[h, at, :], i_ref[h])

    def pick():
        sig_parts = split3(sig_ref[...])
        chosen = pick_ref[...]
        yt[...] = dot_t(chosen, sig_parts[0]) + (dot_t(chosen, sig_parts[1]) + dot_t(chosen, sig_parts[2]))
        at = pl.ds(pl.multiple_of(leaf * sa, sa), sa)

        @pl.loop(0, leaves * group)
        def _(h):
            local = st_ref[h, :, at] - leaf * root_rows
            hot = jnp.where(lax.broadcasted_iota(jnp.int32, (root_rows, sa), 0) == local, 1.0, 0.0).astype(BF16)
            parts = split3(yt[pl.ds(pl.multiple_of(h * ra, ra), ra), :])
            asend[h] = dot(parts[0], hot) + (dot(parts[1], hot) + dot(parts[2], hot))

    def l_copies():
        out = []
        for d in range(1, leaves):
            target = (leaf + d) % leaves
            out.append(copy(
                asend.at[pl.ds(target * group, group)],
                aa.at[:, pl.ds(pl.multiple_of(c * ra, ra), ra), pl.ds(pl.multiple_of(leaf * sa, sa), sa)],
                l_ss.at[d - 1], l_rs.at[d - 1], {"leaf": target},
            ))
        return out

    def product_done(h):
        for k in range(2):
            at = pl.ds(pl.multiple_of(y * tb + k * (tb // 2), tb // 2), tb // 2)
            pf[h, at, :] = pp[h, at, :] + (pr[h, 0, k] + pr[h, 1, k])

    def ancestor_times(h):
        total = dot3(aa[h, :, pl.ds(0, tb)], pf[h, pl.ds(0, tb), :])
        for s in range(1, rows):
            total = total + dot3(aa[h, :, pl.ds(s * tb, tb)], pf[h, pl.ds(s * tb, tb), :])
        sp_ref[h] = -total
        qt[h, y] = total.T

    def right_terms(h):
        nt[h] = it[h] + dot3(qt[h, 0], w_ref[h, pl.ds(0, tb), :])

        @pl.loop(1, rows)
        def _(s):
            nt[h] = nt[h] + dot3(qt[h, s], w_ref[h, pl.ds(pl.multiple_of(s * tb, tb), tb), :])

    def diagonal_partial(h):
        @pl.loop(0, cols)
        def _(slot):
            dp[h, slot] = dot3(nt[h], ig[slot, h])

    def diagonal_done(h):
        for k in range(2):
            total = dp[h, 2 * y + k] + (dr[h, 0, k] + dr[h, 1, k])
            sd_ref[h, pl.ds(k * cb, cb), :] = total.T

    ig[c] = i_ref[...]
    product_partial(0)
    pl.semaphore_wait(barrier, 2 + leaves + (z > 0).astype(jnp.int32) + (z < depth - 1).astype(jnp.int32))

    anc = group
    p0, p1 = p_rs_copies(0), p_rs_copies(1)
    f0, f1 = pf_copies(0), pf_copies(1)
    q0, q1 = qt_copies(0), qt_copies(1)
    d0, d1 = d_rs_copies(0), d_rs_copies(1)
    exchange = l_copies()

    rs_round1(p0)
    z_own(0)
    pick()
    for one in exchange:
        one.start()
    aa[:, pl.ds(pl.multiple_of(c * ra, ra), ra), pl.ds(pl.multiple_of(leaf * sa, sa), sa)] = asend[
        pl.ds(leaf * group, group)
    ]
    product_partial(1)
    rs_round1(p1)
    rs_round2(p0, p_part(0), lambda k: ph.at[0, k])
    for h in range(group):
        it[h] = i_ref[h].T
    for one in exchange:
        one.wait_recv()
    z_own(anc)
    rs_arrived(p0)
    product_done(0)
    ag_round1(f0)
    rs_round2(p1, p_part(1), lambda k: ph.at[1, k])
    rs_arrived(p1)
    product_done(1)
    ag_round1(f1)
    z_relay(anc, 1)
    ag_round2(f0)
    z_relay(anc, 2)
    z_relay(0, 1)
    ag_arrived(f0)
    z_relay(anc, 3)
    z_last(anc)
    ancestor_times(0)
    ag_round1(q0)
    ag_round2(f1)
    ag_arrived(f1)
    ancestor_times(1)
    ag_round1(q1)
    ag_round2(q0)
    z_relay(0, 2)
    z_own(1)
    ag_arrived(q0)
    right_terms(0)
    ag_round2(q1)
    z_relay(0, 3)
    z_last(0)
    diagonal_partial(0)
    rs_round1(d0)
    z_relay(1, 1)
    ag_arrived(q1)
    right_terms(1)
    rs_round2(d0, d_part(0), lambda k: dh.at[0, k])
    z_relay(1, 2)
    z_relay(1, 3)
    z_last(1)
    diagonal_partial(1)
    rs_round1(d1)
    rs_arrived(d0)
    diagonal_done(0)
    rs_round2(d1, d_part(1), lambda k: dh.at[1, k])
    rs_arrived(d1)
    diagonal_done(1)

    for copies in (p0, p1, f0, f1, q0, q1, d0, d1, exchange):
        sent(copies)
    for item in range(group + 1):
        z_sent(item)


def body(sigma_root, structure, inv_diag, panel):
    leaves, rows, cols = lax.axis_size("leaf"), lax.axis_size("row"), lax.axis_size("col")
    group, kb, cb = inv_diag.shape
    ns = panel.shape[1]
    children = structure.shape[0]
    root_rows, root_cols = sigma_root.shape
    ra = ns // (rows * cols)
    sa = ns // leaves
    tb = ns // rows
    grid_pos = lax.axis_index("row") * cols + lax.axis_index("col")
    own_cols = lax.dynamic_slice_in_dim(structure, grid_pos * ra, ra, 1) - grid_pos * root_cols
    pick = (own_cols[:, :, None] == jnp.arange(root_cols, dtype=jnp.int32)[None, None, :]).astype(BF16)
    pick = pick.reshape(children * ra, root_cols)
    dma = pltpu.SemaphoreType.DMA
    vmem = pltpu.VMEM
    items = group + 1
    depth = cols // 2
    return pl.pallas_call(
        partial(kernel, (leaves, rows, cols, group, ns, kb, cb, root_rows)),
        out_shape=(
            jax.ShapeDtypeStruct((group, tb, cb), F32),
            jax.ShapeDtypeStruct((group, kb, cb), F32),
        ),
        in_specs=[pl.BlockSpec(memory_space=vmem)] * 5,
        out_specs=[pl.BlockSpec(memory_space=vmem)] * 2,
        scratch_shapes=[
            vmem((cols, group, kb, cb), F32),
            vmem((group, tb, ns), F32),
            vmem((children, ra, sa), F32),
            vmem((children * ra, root_rows), F32),
            vmem((group, ns, cb), F32),
            vmem((group, 2, tb // 2, cb), F32),
            vmem((group, 2, 2, tb // 2, cb), F32),
            vmem((group, ns, cb), F32),
            vmem((group, rows, cb, tb), F32),
            vmem((group, cb, kb), F32),
            vmem((group, cb, kb), F32),
            vmem((group, cols, cb, cb), F32),
            vmem((group, 2, cb, cb), F32),
            vmem((group, 2, 2, cb, cb), F32),
            dma((items, 2, depth - 1)), dma((items, 2, depth - 1)),
            dma((items, depth)), dma((items, depth)),
            dma((leaves - 1,)), dma((leaves - 1,)),
            dma((group, 6)), dma((group, 6)),
            dma((group, 6)), dma((group, 6)),
            dma((group, 6)), dma((group, 6)),
            dma((group, 6)), dma((group, 6)),
        ],
        compiler_params=pltpu.CompilerParams(
            collective_id=0, has_side_effects=True, vmem_limit_bytes=56 * 1024 * 1024
        ),
    )(panel, inv_diag, sigma_root, structure[:, None, :], pick)


def solution(mesh):
    placed = (P("leaf", ("row", "col")), P(), P("leaf", "row", "col"), P("leaf", None, "row"))
    return jax.shard_map(
        body,
        mesh=mesh,
        in_specs=placed,
        out_specs=(P("leaf", "row", "col"), P("leaf", "row", "col")),
        check_vma=False,
    )
```

```python
from functools import partial

import jax
import jax.numpy as jnp
from jax import lax
from jax.experimental import pallas as pl
from jax.experimental.pallas import tpu as pltpu
from jax.sharding import PartitionSpec as P

MESH = pl.DeviceIdType.MESH
F32 = jnp.float32
BF16 = jnp.bfloat16


def split(x):
    high = x.astype(BF16)
    return high, (x - high.astype(F32)).astype(BF16)


def split3(x):
    high = x.astype(BF16)
    rest = x - high.astype(F32)
    mid = rest.astype(BF16)
    return high, mid, (rest - mid.astype(F32)).astype(BF16)


def dot(a, b):
    return lax.dot_general(a, b, (((1,), (0,)), ((), ())), preferred_element_type=F32)


def dot_t(a, b):
    return lax.dot_general(a, b, (((1,), (1,)), ((), ())), preferred_element_type=F32)


def dot3(a, b):
    ah, al = split(a)
    bh, bl = split(b)
    return dot(ah, bh) + (dot(ah, bl) + dot(al, bh))


def kernel(
    sizes,
    w_ref, i_ref, sig_ref, st_ref, pick_ref,
    sp_ref, sd_ref,
    ig, aa, asend, yt, pp, ph, pr, pf, qt, it, nt, dp, dh, dr,
    ml, z_ss, z_rs, b_ss, b_rs, l_ss, l_rs, p_ss, p_rs, a_ss, a_rs, s_ss, s_rs, d_ss, d_rs, m_ss, m_rs,
):
    leaves, rows, cols, group, ns, kb, cb, root_rows = sizes
    depth = cols // 2
    tb = ns // rows
    ra = ns // (rows * cols)
    sa = ns // leaves
    leaf = lax.axis_index("leaf")
    y = lax.axis_index("row")
    c = lax.axis_index("col")
    z = c // 2
    core = c % 2
    y_next, y_prev, y_far = (y + 1) % rows, (y + rows - 1) % rows, (y + 2) % rows
    sibling = c + 1 - 2 * core

    def copy(src, dst, ss, rs, target):
        return pltpu.make_async_remote_copy(
            src_ref=src, dst_ref=dst, send_sem=ss, recv_sem=rs, device_id=target, device_id_type=MESH
        )

    barrier = pltpu.get_barrier_semaphore()
    for target in ({"row": y_next}, {"row": y_prev}, {"col": sibling}):
        pl.semaphore_signal(barrier, inc=1, device_id=target, device_id_type=MESH)
    for d in range(1, leaves):
        pl.semaphore_signal(barrier, inc=1, device_id={"leaf": (leaf + d) % leaves}, device_id_type=MESH)

    @pl.when(z > 0)
    def _():
        pl.semaphore_signal(barrier, inc=1, device_id={"col": c - 2}, device_id_type=MESH)

    @pl.when(z < depth - 1)
    def _():
        pl.semaphore_signal(barrier, inc=1, device_id={"col": c + 2}, device_id_type=MESH)

    corner = jnp.logical_or(
        jnp.logical_and(y == 0, z == depth - 1), jnp.logical_and(y == rows - 1, z == 0)
    )

    @pl.when(corner)
    def _():
        for k in range(2):
            pl.semaphore_signal(barrier, inc=1, device_id={"row": z, "col": 2 * y + k}, device_id_type=MESH)

    def view(item, slot):
        if item < group:
            return ig.at[slot, item]
        return aa.at[:, pl.ds(pl.multiple_of(slot * ra, ra), ra), :]

    def z_copy(item, way, step):
        slot = c - 2 * (step - 1) if way == 0 else c + 2 * (step - 1)
        target = c + 2 if way == 0 else c - 2
        return copy(
            view(item, slot), view(item, slot),
            z_ss.at[item, way, step - 1], z_rs.at[item, way, step - 1], {"col": target},
        )

    def z_cut(item, way, step):
        return step == depth - 1 and ((item == 0 and way == 1) or (item == 1 and way == 0))

    def z_sends(item, way, step):
        if z_cut(item, way, step):
            return None
        if way == 0:
            cond, origin = jnp.logical_and(z < depth - 1, z >= step - 1), z - step + 1
        else:
            cond, origin = jnp.logical_and(z > 0, z + step - 1 <= depth - 1), z + step - 1
        return jnp.logical_and(cond, origin <= y) if item < group else cond

    def z_gets(item, way, step):
        if z_cut(item, way, step):
            return None
        cond, origin = (z >= step, z - step) if way == 0 else (z + step <= depth - 1, z + step)
        return jnp.logical_and(cond, origin <= y) if item < group else cond

    def when(cond, do):
        if cond is not None:
            pl.when(cond)(do)

    def has_own(item):
        return z <= y if item < group else z >= 0

    def b_copy(item, origin):
        slot = 2 * origin + core
        return copy(view(item, slot), view(item, slot), b_ss.at[item, origin], b_rs.at[item, origin], {"col": sibling})

    def b_landed(item, origin):
        slot = 2 * origin + 1 - core
        copy(
            view(item, slot), view(item, slot), b_ss.at[item, origin], b_rs.at[item, origin], {"col": sibling}
        ).wait_recv()

    def z_start(item, way, step):
        when(z_sends(item, way, step), lambda: z_copy(item, way, step).start())

    def z_own(item):
        z_start(item, 0, 1)
        z_start(item, 1, 1)
        when(has_own(item), lambda: b_copy(item, z).start())

    def z_relay(item, step):
        for way in range(2):
            def relay():
                origin = z - step if way == 0 else z + step
                slot = 2 * origin + core
                copy(
                    view(item, slot), view(item, slot),
                    z_ss.at[item, way, step - 1], z_rs.at[item, way, step - 1], {"col": sibling},
                ).wait_recv()
                if step < depth - 1:
                    z_start(item, way, step + 1)
                b_copy(item, origin).start()

            when(z_gets(item, way, step), relay)

    def z_last(item):
        for origin in range(depth):
            b_landed(item, origin)

    def z_sent(item):
        for way in range(2):
            for step in range(1, depth):
                when(z_sends(item, way, step), lambda: z_copy(item, way, step).wait_send())
                when(z_gets(item, way, step), lambda: b_copy(item, z - step if way == 0 else z + step).wait_send())
        when(has_own(item), lambda: b_copy(item, z).wait_send())

    def rs_copies(part, half, whole, ss, rs):
        right, left = {"row": y_next}, {"row": y_prev}
        plan = (
            (part(y_far, 0), half(0), right),
            (part(y_far, 1), half(1), left),
            (part(y_next, 1), whole(0, 1), right),
            (part(y_prev, 0), whole(1, 0), left),
            (part(y_next, 0), whole(0, 0), right),
            (part(y_prev, 1), whole(1, 1), left),
        )
        return [copy(src, dst, ss.at[k], rs.at[k], target) for k, (src, dst, target) in enumerate(plan)]

    def p_part(h):
        return lambda s, k: pp.at[h, pl.ds(pl.multiple_of(s * tb + k * (tb // 2), tb // 2), tb // 2), :]

    def p_rs_copies(h):
        return rs_copies(
            p_part(h), lambda k: ph.at[h, k],
            lambda w, k: pr.at[h, w, k], p_ss.at[h], p_rs.at[h],
        )

    def d_part(h):
        return lambda s, k: dp.at[h, 2 * s + k]

    def d_rs_copies(h):
        return rs_copies(
            d_part(h), lambda k: dh.at[h, k],
            lambda w, k: dr.at[h, w, k], d_ss.at[h], d_rs.at[h],
        )

    def rs_round1(copies):
        for k in range(4):
            copies[k].start()

    def rs_round2(copies, part, half):
        copies[0].wait_recv()
        mine = part(y_next, 0)
        mine[...] = mine[...] + half(0)[...]
        copies[4].start()
        copies[1].wait_recv()
        mine = part(y_prev, 1)
        mine[...] = mine[...] + half(1)[...]
        copies[5].start()

    def rs_arrived(copies):
        for k in range(2, 6):
            copies[k].wait_recv()

    def sent(copies):
        for one in copies:
            one.wait_send()

    def ag_copies(slot, ss, rs):
        right, left = {"row": y_next}, {"row": y_prev}
        plan = (
            (slot(y, 0), right), (slot(y, 1), left), (slot(y, 1), right), (slot(y, 0), left),
            (slot(y_prev, 0), right), (slot(y_next, 1), left),
        )
        return [copy(src, src, ss.at[k], rs.at[k], target) for k, (src, target) in enumerate(plan)]

    def pf_copies(h):
        slot = lambda s, k: pf.at[h, pl.ds(pl.multiple_of(s * tb + k * (tb // 2), tb // 2), tb // 2), :]
        return ag_copies(slot, a_ss.at[h], a_rs.at[h])

    def qt_copies(h):
        slot = lambda s, k: qt.at[h, s, pl.ds(k * (cb // 2), cb // 2), :]
        return ag_copies(slot, s_ss.at[h], s_rs.at[h])

    def ag_round1(copies):
        for k in range(4):
            copies[k].start()

    def ag_round2(copies):
        copies[0].wait_recv()
        copies[4].start()
        copies[1].wait_recv()
        copies[5].start()

    def ag_arrived(copies):
        for k in range(2, 6):
            copies[k].wait_recv()

    def product_partial(h):
        @pl.loop(0, rows)
        def _(s):
            at = pl.ds(pl.multiple_of(s * tb, tb), tb)
            pp[h, at, :] = dot3(w_ref[h, at, :], i_ref[h])

    def pick():
        sig_parts = split3(sig_ref[...])
        chosen = pick_ref[...]
        yt[...] = dot_t(chosen, sig_parts[0]) + (dot_t(chosen, sig_parts[1]) + dot_t(chosen, sig_parts[2]))
        at = pl.ds(pl.multiple_of(leaf * sa, sa), sa)

        @pl.loop(0, leaves * group)
        def _(h):
            local = st_ref[h, :, at] - leaf * root_rows
            hot = jnp.where(lax.broadcasted_iota(jnp.int32, (root_rows, sa), 0) == local, 1.0, 0.0).astype(BF16)
            parts = split3(yt[pl.ds(pl.multiple_of(h * ra, ra), ra), :])
            asend[h] = dot(parts[0], hot) + (dot(parts[1], hot) + dot(parts[2], hot))

    def l_copies():
        out = []
        for d in range(1, leaves):
            target = (leaf + d) % leaves
            out.append(copy(
                asend.at[pl.ds(target * group, group)],
                aa.at[:, pl.ds(pl.multiple_of(c * ra, ra), ra), pl.ds(pl.multiple_of(leaf * sa, sa), sa)],
                l_ss.at[d - 1], l_rs.at[d - 1], {"leaf": target},
            ))
        return out

    def product_done(h):
        for k in range(2):
            at = pl.ds(pl.multiple_of(y * tb + k * (tb // 2), tb // 2), tb // 2)
            pf[h, at, :] = pp[h, at, :] + (pr[h, 0, k] + pr[h, 1, k])

    def ancestor_times(h):
        total = dot3(aa[h, :, pl.ds(0, tb)], pf[h, pl.ds(0, tb), :])
        for s in range(1, rows):
            total = total + dot3(aa[h, :, pl.ds(s * tb, tb)], pf[h, pl.ds(s * tb, tb), :])
        sp_ref[h] = -total
        qt[h, y] = total.T

    def right_terms(h):
        nt[h] = it[h] + dot3(qt[h, 0], w_ref[h, pl.ds(0, tb), :])

        @pl.loop(1, rows)
        def _(s):
            nt[h] = nt[h] + dot3(qt[h, s], w_ref[h, pl.ds(pl.multiple_of(s * tb, tb), tb), :])

    def uncut(h):
        return z < depth - 1 if h == 1 else z >= 0

    def d_goes(h):
        late = jnp.logical_or(y >= 2, jnp.logical_and(y == 1, uncut(h)))
        far = jnp.logical_or(y == 3, jnp.logical_and(y == 2, uncut(h)))
        wrap = jnp.logical_and(y == 3, uncut(h))
        return (far, far, wrap, late, jnp.logical_or(y == 0, wrap), late)

    def diagonal_slice(h, copies, origin):
        b_landed(h, origin)
        for k in range(2):
            dp[h, 2 * origin + k] = dot3(nt[h], ig[2 * origin + k, h])

        @pl.when(origin == y_far)
        def _():
            copies[0].start()
            copies[1].start()

        @pl.when(origin == y_next)
        def _():
            copies[2].start()

        @pl.when(origin == y_prev)
        def _():
            copies[3].start()

            @pl.when(y == 3)
            def _():
                copies[5].start()

    def diagonal_step(h, copies, step):
        if step == 0:
            when(z <= y, lambda: diagonal_slice(h, copies, z))
            return
        for way in range(2):
            when(z_gets(h, way, step), lambda: diagonal_slice(h, copies, z - step if way == 0 else z + step))

    def d_round2(h, copies):
        @pl.when(jnp.logical_and(y == 3, uncut(h)))
        def _():
            copies[0].wait_recv()
            dp[h, 0] = dp[h, 0] + dh[h, 0]
            copies[4].start()

        @pl.when(y == 0)
        def _():
            copies[0].wait_recv()
            dp[h, 2] = dh[h, 0]
            copies[4].start()

        @pl.when(jnp.logical_or(y == 2, jnp.logical_and(y == 1, uncut(h))))
        def _():
            copies[1].wait_recv()
            mine = d_part(h)(y_prev, 1)
            mine[...] = mine[...] + dh[h, 1]
            copies[5].start()

    def d_finish(h, copies):
        first = jnp.logical_and(y == 0, uncut(h))
        middle = jnp.logical_or(y == 1, y == 2)

        @pl.when(jnp.logical_or(first, middle))
        def _():
            copies[3].wait_recv()
            dp[h, 2 * y] = dp[h, 2 * y] + dr[h, 1, 0]

        @pl.when(jnp.logical_or(first, y == 1))
        def _():
            copies[4].wait_recv()
            dp[h, 2 * y] = dp[h, 2 * y] + dr[h, 0, 0]

        @pl.when(first)
        def _():
            copies[2].wait_recv()
            dp[h, 2 * y + 1] = dp[h, 2 * y + 1] + dr[h, 0, 1]

        @pl.when(jnp.logical_or(first, middle))
        def _():
            copies[5].wait_recv()
            dp[h, 2 * y + 1] = dp[h, 2 * y + 1] + dr[h, 1, 1]

        mirrored = jnp.logical_and(corner, (y == 3) if h == 0 else (y == 0))

        @pl.when(jnp.logical_not(mirrored))
        def _():
            for k in range(2):
                sd_ref[h, pl.ds(k * cb, cb), :] = dp[h, 2 * y + k].T

    def m_copy(h, k):
        return copy(dp.at[h, 2 * y + k], ml.at[core], m_ss.at[k], m_rs.at[core], {"row": z, "col": 2 * y + k})

    def m_sends(h):
        return jnp.logical_and(corner, (y == 0) if h == 0 else (y == 3))

    def m_start(h):
        @pl.when(m_sends(h))
        def _():
            for k in range(2):
                m_copy(h, k).start()

    def m_finish(h):
        @pl.when(jnp.logical_and(corner, (y == 3) if h == 0 else (y == 0)))
        def _():
            for k in range(2):
                copy(ml.at[k], ml.at[k], m_ss.at[k], m_rs.at[k], {"row": z}).wait_recv()
                sd_ref[h, pl.ds(k * cb, cb), :] = ml[k]

        @pl.when(m_sends(h))
        def _():
            for k in range(2):
                m_copy(h, k).wait_send()

    ig[c] = i_ref[...]
    product_partial(0)
    pick()
    pl.semaphore_wait(barrier, 2 + leaves + (z > 0).astype(jnp.int32) + (z < depth - 1).astype(jnp.int32)
        + 2 * corner.astype(jnp.int32))

    anc = group
    p0, p1 = p_rs_copies(0), p_rs_copies(1)
    f0, f1 = pf_copies(0), pf_copies(1)
    q0, q1 = qt_copies(0), qt_copies(1)
    d0, d1 = d_rs_copies(0), d_rs_copies(1)
    exchange = l_copies()

    rs_round1(p0)
    for one in exchange:
        one.start()
    aa[:, pl.ds(pl.multiple_of(c * ra, ra), ra), pl.ds(pl.multiple_of(leaf * sa, sa), sa)] = asend[
        pl.ds(leaf * group, group)
    ]
    z_own(0)
    rs_round2(p0, p_part(0), lambda k: ph.at[0, k])
    rs_arrived(p0)
    product_done(0)
    ag_round1(f0)
    product_partial(1)
    rs_round1(p1)
    for one in exchange:
        one.wait_recv()
    z_own(anc)
    ag_round2(f0)
    z_relay(anc, 1)
    rs_round2(p1, p_part(1), lambda k: ph.at[1, k])
    rs_arrived(p1)
    product_done(1)
    ag_round1(f1)
    z_relay(anc, 2)
    ag_round2(f1)
    z_relay(anc, 3)
    ag_arrived(f0)
    z_last(anc)
    ancestor_times(0)
    ag_round1(q0)
    z_relay(0, 1)
    ag_round2(q0)
    for h in range(group):
        it[h] = i_ref[h].T
    ag_arrived(f1)
    ancestor_times(1)
    ag_round1(q1)
    z_relay(0, 2)
    ag_arrived(q0)
    right_terms(0)
    z_own(1)
    ag_round2(q1)
    diagonal_step(0, d0, 0)
    diagonal_step(0, d0, 1)
    z_relay(0, 3)
    diagonal_step(0, d0, 2)
    diagonal_step(0, d0, 3)
    ag_arrived(q1)
    right_terms(1)
    z_relay(1, 1)
    diagonal_step(1, d1, 0)
    diagonal_step(1, d1, 1)
    d_round2(0, d0)
    z_relay(1, 2)
    diagonal_step(1, d1, 2)
    d_finish(0, d0)
    m_start(0)
    z_relay(1, 3)
    diagonal_step(1, d1, 3)
    m_start(1)
    d_round2(1, d1)
    d_finish(1, d1)
    m_finish(0)
    m_finish(1)

    for copies in (p0, p1, f0, f1, q0, q1, exchange):
        sent(copies)
    for h, copies in enumerate((d0, d1)):
        for cond, one in zip(d_goes(h), copies):
            when(cond, one.wait_send)
    for item in range(group + 1):
        z_sent(item)


def body(sigma_root, structure, inv_diag, panel):
    leaves, rows, cols = lax.axis_size("leaf"), lax.axis_size("row"), lax.axis_size("col")
    group, kb, cb = inv_diag.shape
    ns = panel.shape[1]
    children = structure.shape[0]
    root_rows, root_cols = sigma_root.shape
    ra = ns // (rows * cols)
    sa = ns // leaves
    tb = ns // rows
    grid_pos = lax.axis_index("row") * cols + lax.axis_index("col")
    own_cols = lax.dynamic_slice_in_dim(structure, grid_pos * ra, ra, 1) - grid_pos * root_cols
    pick = (own_cols[:, :, None] == jnp.arange(root_cols, dtype=jnp.int32)[None, None, :]).astype(BF16)
    pick = pick.reshape(children * ra, root_cols)
    dma = pltpu.SemaphoreType.DMA
    vmem = pltpu.VMEM
    items = group + 1
    depth = cols // 2
    return pl.pallas_call(
        partial(kernel, (leaves, rows, cols, group, ns, kb, cb, root_rows)),
        out_shape=(
            jax.ShapeDtypeStruct((group, tb, cb), F32),
            jax.ShapeDtypeStruct((group, kb, cb), F32),
        ),
        in_specs=[pl.BlockSpec(memory_space=vmem)] * 5,
        out_specs=[pl.BlockSpec(memory_space=vmem)] * 2,
        scratch_shapes=[
            vmem((cols, group, kb, cb), F32),
            vmem((group, tb, ns), F32),
            vmem((children, ra, sa), F32),
            vmem((children * ra, root_rows), F32),
            vmem((group, ns, cb), F32),
            vmem((group, 2, tb // 2, cb), F32),
            vmem((group, 2, 2, tb // 2, cb), F32),
            vmem((group, ns, cb), F32),
            vmem((group, rows, cb, tb), F32),
            vmem((group, cb, kb), F32),
            vmem((group, cb, kb), F32),
            vmem((group, cols, cb, cb), F32),
            vmem((group, 2, cb, cb), F32),
            vmem((group, 2, 2, cb, cb), F32),
            vmem((2, cb, cb), F32),
            dma((items, 2, depth - 1)), dma((items, 2, depth - 1)),
            dma((items, depth)), dma((items, depth)),
            dma((leaves - 1,)), dma((leaves - 1,)),
            dma((group, 6)), dma((group, 6)),
            dma((group, 6)), dma((group, 6)),
            dma((group, 6)), dma((group, 6)),
            dma((group, 6)), dma((group, 6)),
            dma((2,)), dma((2,)),
        ],
        compiler_params=pltpu.CompilerParams(
            collective_id=0, has_side_effects=True, vmem_limit_bytes=56 * 1024 * 1024
        ),
    )(panel, inv_diag, sigma_root, structure[:, None, :], pick)


def solution(mesh):
    placed = (P("leaf", ("row", "col")), P(), P("leaf", "row", "col"), P("leaf", None, "row"))
    return jax.shard_map(
        body,
        mesh=mesh,
        in_specs=placed,
        out_specs=(P("leaf", "row", "col"), P("leaf", "row", "col")),
        check_vma=False,
    )
```

```python
from functools import partial

import jax
import jax.numpy as jnp
from jax import lax
from jax.experimental import pallas as pl
from jax.experimental.pallas import tpu as pltpu
from jax.sharding import PartitionSpec as P

MESH = pl.DeviceIdType.MESH
F32 = jnp.float32
BF16 = jnp.bfloat16


def split(x):
    high = x.astype(BF16)
    return high, (x - high.astype(F32)).astype(BF16)


def dot(a, b):
    return lax.dot_general(a, b, (((1,), (0,)), ((), ())), preferred_element_type=F32)


def dot_t(a, b):
    return lax.dot_general(a, b, (((1,), (1,)), ((), ())), preferred_element_type=F32)


def dot3(a, b):
    ah, al = split(a)
    bh, bl = split(b)
    return dot(ah, bh) + (dot(ah, bl) + dot(al, bh))


def kernel(
    sizes,
    w_hbm, i_ref, sig_hbm, st_ref,
    sp_ref, sd_ref,
    w_ref, sig_ref, ig, aa, asend, hot_col, col_idx, row_idx, yt, pp, ph, pr, pf, qt, it, nt, dp, dh, dr,
    ml, z_ss, z_rs, b_ss, b_rs, l_ss, l_rs, p_ss, p_rs, a_ss, a_rs, s_ss, s_rs, d_ss, d_rs, m_ss, m_rs, in_sem,
):
    leaves, rows, cols, group, ns, kb, cb, root_rows, root_cols = sizes
    depth = cols // 2
    tb = ns // rows
    ra = ns // (rows * cols)
    sa = ns // leaves
    leaf = lax.axis_index("leaf")
    y = lax.axis_index("row")
    c = lax.axis_index("col")
    z = c // 2
    core = c % 2
    y_next, y_prev, y_far = (y + 1) % rows, (y + rows - 1) % rows, (y + 2) % rows
    sibling = c + 1 - 2 * core

    def copy(src, dst, ss, rs, target):
        return pltpu.make_async_remote_copy(
            src_ref=src, dst_ref=dst, send_sem=ss, recv_sem=rs, device_id=target, device_id_type=MESH
        )

    fetch = [pltpu.make_async_copy(w_hbm.at[h], w_ref.at[h], in_sem.at[h]) for h in range(group)]
    fetch_root = pltpu.make_async_copy(sig_hbm, sig_ref, in_sem.at[group])
    fetch[0].start()
    fetch_root.start()
    fetch[1].start()

    barrier = pltpu.get_barrier_semaphore()
    for target in ({"row": y_next}, {"row": y_prev}, {"col": sibling}):
        pl.semaphore_signal(barrier, inc=1, device_id=target, device_id_type=MESH)
    for d in range(1, leaves):
        pl.semaphore_signal(barrier, inc=1, device_id={"leaf": (leaf + d) % leaves}, device_id_type=MESH)

    @pl.when(z > 0)
    def _():
        pl.semaphore_signal(barrier, inc=1, device_id={"col": c - 2}, device_id_type=MESH)

    @pl.when(z < depth - 1)
    def _():
        pl.semaphore_signal(barrier, inc=1, device_id={"col": c + 2}, device_id_type=MESH)

    corner = jnp.logical_or(
        jnp.logical_and(y == 0, z == depth - 1), jnp.logical_and(y == rows - 1, z == 0)
    )

    @pl.when(corner)
    def _():
        for k in range(2):
            pl.semaphore_signal(barrier, inc=1, device_id={"row": z, "col": 2 * y + k}, device_id_type=MESH)

    def view(item, slot):
        if item < group:
            return ig.at[slot, item]
        return aa.at[item - group, pl.ds(pl.multiple_of(slot * ra, ra), ra), :]

    def z_copy(item, way, step):
        slot = c - 2 * (step - 1) if way == 0 else c + 2 * (step - 1)
        target = c + 2 if way == 0 else c - 2
        return copy(
            view(item, slot), view(item, slot),
            z_ss.at[item, way, step - 1], z_rs.at[item, way, step - 1], {"col": target},
        )

    def z_cut(item, way, step):
        return step == depth - 1 and ((item == 0 and way == 1) or (item == 1 and way == 0))

    def z_sends(item, way, step):
        if z_cut(item, way, step):
            return None
        if way == 0:
            cond, origin = jnp.logical_and(z < depth - 1, z >= step - 1), z - step + 1
        else:
            cond, origin = jnp.logical_and(z > 0, z + step - 1 <= depth - 1), z + step - 1
        return jnp.logical_and(cond, origin <= y) if item < group else cond

    def z_gets(item, way, step):
        if z_cut(item, way, step):
            return None
        cond, origin = (z >= step, z - step) if way == 0 else (z + step <= depth - 1, z + step)
        return jnp.logical_and(cond, origin <= y) if item < group else cond

    def when(cond, do):
        if cond is not None:
            pl.when(cond)(do)

    def has_own(item):
        return z <= y if item < group else z >= 0

    def b_copy(item, origin):
        slot = 2 * origin + core
        return copy(view(item, slot), view(item, slot), b_ss.at[item, origin], b_rs.at[item, origin], {"col": sibling})

    def b_landed(item, origin):
        slot = 2 * origin + 1 - core
        copy(
            view(item, slot), view(item, slot), b_ss.at[item, origin], b_rs.at[item, origin], {"col": sibling}
        ).wait_recv()

    def z_start(item, way, step):
        when(z_sends(item, way, step), lambda: z_copy(item, way, step).start())

    def z_own(item):
        z_start(item, 0, 1)
        z_start(item, 1, 1)
        when(has_own(item), lambda: b_copy(item, z).start())

    def z_relay(item, step):
        for way in range(2):
            def relay():
                origin = z - step if way == 0 else z + step
                slot = 2 * origin + core
                copy(
                    view(item, slot), view(item, slot),
                    z_ss.at[item, way, step - 1], z_rs.at[item, way, step - 1], {"col": sibling},
                ).wait_recv()
                if step < depth - 1:
                    z_start(item, way, step + 1)
                b_copy(item, origin).start()

            when(z_gets(item, way, step), relay)

    def z_last(item):
        for origin in range(depth):
            b_landed(item, origin)

    def z_sent(item):
        for way in range(2):
            for step in range(1, depth):
                when(z_sends(item, way, step), lambda: z_copy(item, way, step).wait_send())
                when(z_gets(item, way, step), lambda: b_copy(item, z - step if way == 0 else z + step).wait_send())
        when(has_own(item), lambda: b_copy(item, z).wait_send())

    def rs_copies(part, half, whole, ss, rs):
        right, left = {"row": y_next}, {"row": y_prev}
        plan = (
            (part(y_far, 0), half(0), right),
            (part(y_far, 1), half(1), left),
            (part(y_next, 1), whole(0, 1), right),
            (part(y_prev, 0), whole(1, 0), left),
            (part(y_next, 0), whole(0, 0), right),
            (part(y_prev, 1), whole(1, 1), left),
        )
        return [copy(src, dst, ss.at[k], rs.at[k], target) for k, (src, dst, target) in enumerate(plan)]

    def p_part(h):
        return lambda s, k: pp.at[h, pl.ds(pl.multiple_of(s * tb + k * (tb // 2), tb // 2), tb // 2), :]

    def p_rs_copies(h):
        return rs_copies(
            p_part(h), lambda k: ph.at[h, k],
            lambda w, k: pr.at[h, w, k], p_ss.at[h], p_rs.at[h],
        )

    def d_part(h):
        return lambda s, k: dp.at[h, 2 * s + k]

    def d_rs_copies(h):
        return rs_copies(
            d_part(h), lambda k: dh.at[h, k],
            lambda w, k: dr.at[h, w, k], d_ss.at[h], d_rs.at[h],
        )

    def rs_round1(copies):
        for k in range(4):
            copies[k].start()

    def rs_round2(copies, part, half):
        copies[0].wait_recv()
        mine = part(y_next, 0)
        mine[...] = mine[...] + half(0)[...]
        copies[4].start()
        copies[1].wait_recv()
        mine = part(y_prev, 1)
        mine[...] = mine[...] + half(1)[...]
        copies[5].start()

    def rs_arrived(copies):
        for k in range(2, 6):
            copies[k].wait_recv()

    def sent(copies):
        for one in copies:
            one.wait_send()

    def ag_copies(slot, ss, rs):
        right, left = {"row": y_next}, {"row": y_prev}
        plan = (
            (slot(y, 0), right), (slot(y, 1), left), (slot(y, 1), right), (slot(y, 0), left),
            (slot(y_prev, 0), right), (slot(y_next, 1), left),
        )
        return [copy(src, src, ss.at[k], rs.at[k], target) for k, (src, target) in enumerate(plan)]

    def pf_copies(h):
        slot = lambda s, k: pf.at[h, pl.ds(pl.multiple_of(s * tb + k * (tb // 2), tb // 2), tb // 2), :]
        return ag_copies(slot, a_ss.at[h], a_rs.at[h])

    def qt_copies(h):
        slot = lambda s, k: qt.at[h, s, pl.ds(k * (cb // 2), cb // 2), :]
        return ag_copies(slot, s_ss.at[h], s_rs.at[h])

    def ag_round1(copies):
        for k in range(4):
            copies[k].start()

    def ag_round2(copies):
        copies[0].wait_recv()
        copies[4].start()
        copies[1].wait_recv()
        copies[5].start()

    def ag_arrived(copies):
        for k in range(2, 6):
            copies[k].wait_recv()

    def product_partial(h):
        fetch[h].wait()

        @pl.loop(0, rows)
        def _(s):
            at = pl.ds(pl.multiple_of(s * tb, tb), tb)
            pp[h, at, :] = dot3(w_ref[h, at, :], i_ref[h])

    def pick():
        fetch_root.wait()
        place = y * cols + c
        share = pl.multiple_of((place * ra) // 128 * 128, 128)
        col_idx[...] = st_ref[:, pl.ds(share, min(128, ns))].T - place * root_cols
        mine = col_idx[pl.ds(pl.multiple_of(place * ra - share, ra), ra), :]
        at = pl.ds(pl.multiple_of(leaf * sa, sa), sa)
        lanes = lax.broadcasted_iota(jnp.int32, (ra, root_cols), 1)
        for h in range(leaves * group):
            row_idx[h] = st_ref[pl.ds(h, 1), at] - leaf * root_rows
            hot_col[pl.ds(h * ra, ra), :] = jnp.where(lanes == mine[:, h : h + 1], 1.0, 0.0).astype(BF16)
        high, low = split(sig_ref[...])
        chosen = hot_col[...]
        yt[0] = dot_t(chosen, high).astype(BF16)
        yt[1] = dot_t(chosen, low).astype(BF16)
        sublanes = lax.broadcasted_iota(jnp.int32, (root_rows, sa), 0)

        @pl.loop(0, leaves * group)
        def _(h):
            hot = jnp.where(sublanes == row_idx[h], 1.0, 0.0).astype(BF16)
            mine = pl.ds(pl.multiple_of(h * ra, ra), ra)
            both = dot(jnp.concatenate([yt[0, mine, :], yt[1, mine, :]], axis=0), hot)
            asend[h] = both[:ra] + both[ra:]

    def l_copies():
        out = []
        for d in range(1, leaves):
            target = (leaf + d) % leaves
            out.append(copy(
                asend.at[pl.ds(target * group, group)],
                aa.at[:, pl.ds(pl.multiple_of(c * ra, ra), ra), pl.ds(pl.multiple_of(leaf * sa, sa), sa)],
                l_ss.at[d - 1], l_rs.at[d - 1], {"leaf": target},
            ))
        return out

    def product_done(h):
        for k in range(2):
            at = pl.ds(pl.multiple_of(y * tb + k * (tb // 2), tb // 2), tb // 2)
            pf[h, at, :] = pp[h, at, :] + (pr[h, 0, k] + pr[h, 1, k])

    def ancestor_times(h):
        total = dot3(aa[h, :, pl.ds(0, tb)], pf[h, pl.ds(0, tb), :])
        for s in range(1, rows):
            total = total + dot3(aa[h, :, pl.ds(s * tb, tb)], pf[h, pl.ds(s * tb, tb), :])
        sp_ref[h] = -total
        qt[h, y] = total.T

    def right_terms(h):
        nt[h] = it[h] + dot3(qt[h, 0], w_ref[h, pl.ds(0, tb), :])

        @pl.loop(1, rows)
        def _(s):
            nt[h] = nt[h] + dot3(qt[h, s], w_ref[h, pl.ds(pl.multiple_of(s * tb, tb), tb), :])

    def uncut(h):
        return z < depth - 1 if h == 1 else z >= 0

    def d_goes(h):
        late = jnp.logical_or(y >= 2, jnp.logical_and(y == 1, uncut(h)))
        far = jnp.logical_or(y == 3, jnp.logical_and(y == 2, uncut(h)))
        wrap = jnp.logical_and(y == 3, uncut(h))
        return (far, far, wrap, late, jnp.logical_or(y == 0, wrap), late)

    def diagonal_slice(h, copies, origin):
        b_landed(h, origin)
        for k in range(2):
            dp[h, 2 * origin + k] = dot3(nt[h], ig[2 * origin + k, h])

        @pl.when(origin == y_far)
        def _():
            copies[0].start()
            copies[1].start()

        @pl.when(origin == y_next)
        def _():
            copies[2].start()

        @pl.when(origin == y_prev)
        def _():
            copies[3].start()

            @pl.when(y == 3)
            def _():
                copies[5].start()

    def diagonal_step(h, copies, step):
        if step == 0:
            when(z <= y, lambda: diagonal_slice(h, copies, z))
            return
        for way in range(2):
            when(z_gets(h, way, step), lambda: diagonal_slice(h, copies, z - step if way == 0 else z + step))

    def d_round2(h, copies):
        @pl.when(jnp.logical_and(y == 3, uncut(h)))
        def _():
            copies[0].wait_recv()
            dp[h, 0] = dp[h, 0] + dh[h, 0]
            copies[4].start()

        @pl.when(y == 0)
        def _():
            copies[0].wait_recv()
            dp[h, 2] = dh[h, 0]
            copies[4].start()

        @pl.when(jnp.logical_or(y == 2, jnp.logical_and(y == 1, uncut(h))))
        def _():
            copies[1].wait_recv()
            mine = d_part(h)(y_prev, 1)
            mine[...] = mine[...] + dh[h, 1]
            copies[5].start()

    def d_finish(h, copies):
        first = jnp.logical_and(y == 0, uncut(h))
        middle = jnp.logical_or(y == 1, y == 2)

        @pl.when(jnp.logical_or(first, middle))
        def _():
            copies[3].wait_recv()
            dp[h, 2 * y] = dp[h, 2 * y] + dr[h, 1, 0]

        @pl.when(jnp.logical_or(first, y == 1))
        def _():
            copies[4].wait_recv()
            dp[h, 2 * y] = dp[h, 2 * y] + dr[h, 0, 0]

        @pl.when(first)
        def _():
            copies[2].wait_recv()
            dp[h, 2 * y + 1] = dp[h, 2 * y + 1] + dr[h, 0, 1]

        @pl.when(jnp.logical_or(first, middle))
        def _():
            copies[5].wait_recv()
            dp[h, 2 * y + 1] = dp[h, 2 * y + 1] + dr[h, 1, 1]

        mirrored = jnp.logical_and(corner, (y == 3) if h == 0 else (y == 0))

        @pl.when(jnp.logical_not(mirrored))
        def _():
            for k in range(2):
                sd_ref[h, pl.ds(k * cb, cb), :] = dp[h, 2 * y + k].T

    def m_copy(h, k):
        return copy(dp.at[h, 2 * y + k], ml.at[core], m_ss.at[k], m_rs.at[core], {"row": z, "col": 2 * y + k})

    def m_sends(h):
        return jnp.logical_and(corner, (y == 0) if h == 0 else (y == 3))

    def m_start(h):
        @pl.when(m_sends(h))
        def _():
            for k in range(2):
                m_copy(h, k).start()

    def m_finish(h):
        @pl.when(jnp.logical_and(corner, (y == 3) if h == 0 else (y == 0)))
        def _():
            for k in range(2):
                copy(ml.at[k], ml.at[k], m_ss.at[k], m_rs.at[k], {"row": z}).wait_recv()
                sd_ref[h, pl.ds(k * cb, cb), :] = ml[k]

        @pl.when(m_sends(h))
        def _():
            for k in range(2):
                m_copy(h, k).wait_send()

    p0, p1 = p_rs_copies(0), p_rs_copies(1)
    f0, f1 = pf_copies(0), pf_copies(1)
    q0, q1 = qt_copies(0), qt_copies(1)
    d0, d1 = d_rs_copies(0), d_rs_copies(1)
    exchange = l_copies()

    ig[c] = i_ref[...]
    product_partial(0)
    pick()
    pl.semaphore_wait(barrier, 2 + leaves + (z > 0).astype(jnp.int32) + (z < depth - 1).astype(jnp.int32)
        + 2 * corner.astype(jnp.int32))
    for one in exchange:
        one.start()
    aa[:, pl.ds(pl.multiple_of(c * ra, ra), ra), pl.ds(pl.multiple_of(leaf * sa, sa), sa)] = asend[
        pl.ds(leaf * group, group)
    ]
    rs_round1(p0)
    z_own(0)
    rs_round2(p0, p_part(0), lambda k: ph.at[0, k])
    rs_arrived(p0)
    product_done(0)
    ag_round1(f0)
    product_partial(1)
    rs_round1(p1)
    for one in exchange:
        one.wait_recv()
    z_own(2)
    z_own(3)
    ag_round2(f0)
    z_relay(2, 1)
    z_relay(2, 2)
    rs_round2(p1, p_part(1), lambda k: ph.at[1, k])
    rs_arrived(p1)
    product_done(1)
    ag_round1(f1)
    z_relay(3, 1)
    z_relay(2, 3)
    ag_arrived(f0)
    z_last(2)
    ancestor_times(0)
    ag_round1(q0)
    z_relay(0, 1)
    ag_round2(f1)
    z_relay(3, 2)
    ag_round2(q0)
    for h in range(group):
        it[h] = i_ref[h].T
    z_relay(3, 3)
    ag_arrived(f1)
    z_last(3)
    ancestor_times(1)
    ag_round1(q1)
    z_relay(0, 2)
    ag_arrived(q0)
    right_terms(0)
    z_own(1)
    ag_round2(q1)
    diagonal_step(0, d0, 0)
    diagonal_step(0, d0, 1)
    z_relay(0, 3)
    diagonal_step(0, d0, 2)
    diagonal_step(0, d0, 3)
    ag_arrived(q1)
    right_terms(1)
    z_relay(1, 1)
    diagonal_step(1, d1, 0)
    diagonal_step(1, d1, 1)
    d_round2(0, d0)
    z_relay(1, 2)
    diagonal_step(1, d1, 2)
    d_finish(0, d0)
    m_start(0)
    z_relay(1, 3)
    diagonal_step(1, d1, 3)
    m_start(1)
    d_round2(1, d1)
    d_finish(1, d1)
    m_finish(0)
    m_finish(1)

    for copies in (p0, p1, f0, f1, q0, q1, exchange):
        sent(copies)
    for h, copies in enumerate((d0, d1)):
        for cond, one in zip(d_goes(h), copies):
            when(cond, one.wait_send)
    for item in range(2 * group):
        z_sent(item)


def hand_over(sp_in, sd_in, sp_out, sd_out):
    sp_out[...] = sp_in[...]
    sd_out[...] = sd_in[...]


def body(sigma_root, structure, inv_diag, panel):
    leaves, rows, cols = lax.axis_size("leaf"), lax.axis_size("row"), lax.axis_size("col")
    group, kb, cb = inv_diag.shape
    ns = panel.shape[1]
    children = structure.shape[0]
    root_rows, root_cols = sigma_root.shape
    ra = ns // (rows * cols)
    sa = ns // leaves
    tb = ns // rows
    dma = pltpu.SemaphoreType.DMA
    vmem = pltpu.VMEM
    items = 2 * group
    depth = cols // 2
    made = pl.pallas_call(
        partial(kernel, (leaves, rows, cols, group, ns, kb, cb, root_rows, root_cols)),
        out_shape=(
            jax.ShapeDtypeStruct((group, tb, cb), F32),
            jax.ShapeDtypeStruct((group, kb, cb), F32),
        ),
        in_specs=[pl.BlockSpec(memory_space=kind) for kind in (pl.ANY, vmem, pl.ANY, vmem)],
        out_specs=[pl.BlockSpec(memory_space=vmem)] * 2,
        scratch_shapes=[
            vmem(panel.shape, F32),
            vmem(sigma_root.shape, F32),
            vmem((cols, group, kb, cb), F32),
            vmem((group, tb, ns), F32),
            vmem((children, ra, sa), F32),
            vmem((children * ra, root_cols), BF16),
            vmem((min(128, ns), children), jnp.int32),
            vmem((children, 1, sa), jnp.int32),
            vmem((2, children * ra, root_rows), BF16),
            vmem((group, ns, cb), F32),
            vmem((group, 2, tb // 2, cb), F32),
            vmem((group, 2, 2, tb // 2, cb), F32),
            vmem((group, ns, cb), F32),
            vmem((group, rows, cb, tb), F32),
            vmem((group, cb, kb), F32),
            vmem((group, cb, kb), F32),
            vmem((group, cols, cb, cb), F32),
            vmem((group, 2, cb, cb), F32),
            vmem((group, 2, 2, cb, cb), F32),
            vmem((2, cb, cb), F32),
            dma((items, 2, depth - 1)), dma((items, 2, depth - 1)),
            dma((items, depth)), dma((items, depth)),
            dma((leaves - 1,)), dma((leaves - 1,)),
            dma((group, 6)), dma((group, 6)),
            dma((group, 6)), dma((group, 6)),
            dma((group, 6)), dma((group, 6)),
            dma((group, 6)), dma((group, 6)),
            dma((2,)), dma((2,)),
            dma((group + 1,)),
        ],
        compiler_params=pltpu.CompilerParams(
            collective_id=0, has_side_effects=True, vmem_limit_bytes=56 * 1024 * 1024
        ),
    )(panel, inv_diag, sigma_root, structure)
    return pl.pallas_call(
        hand_over, out_shape=tuple(jax.ShapeDtypeStruct(one.shape, one.dtype) for one in made)
    )(*made)


def solution(mesh):
    placed = (P("leaf", ("row", "col")), P(), P("leaf", "row", "col"), P("leaf", None, "row"))
    return jax.shard_map(
        body,
        mesh=mesh,
        in_specs=placed,
        out_specs=(P("leaf", "row", "col"), P("leaf", "row", "col")),
        check_vma=False,
    )
```

```python
from functools import partial

import jax
import jax.numpy as jnp
from jax import lax
from jax.experimental import pallas as pl
from jax.experimental.pallas import tpu as pltpu
from jax.sharding import PartitionSpec as P

MESH = pl.DeviceIdType.MESH
F32 = jnp.float32
BF16 = jnp.bfloat16


def split(x):
    high = x.astype(BF16)
    return high, (x - high.astype(F32)).astype(BF16)


def dot(a, b):
    return lax.dot_general(a, b, (((1,), (0,)), ((), ())), preferred_element_type=F32)


def dot_t(a, b):
    return lax.dot_general(a, b, (((1,), (1,)), ((), ())), preferred_element_type=F32)


def dot3(a, b):
    ah, al = split(a)
    bh, bl = split(b)
    return dot(ah, bh) + (dot(ah, bl) + dot(al, bh))


def kernel(
    sizes,
    w_hbm, i_ref, sig_hbm, st_ref,
    sp_ref, sd_ref,
    w_ref, sig_ref, ig, aa, asend, hot_col, col_idx, row_idx, yt, pp, ph, pr, pf, qt, it, nt, dp, dh, dr,
    ml, z_ss, z_rs, b_ss, b_rs, l_ss, l_rs, p_ss, p_rs, a_ss, a_rs, s_ss, s_rs, d_ss, d_rs, m_ss, m_rs, in_sem,
):
    leaves, rows, cols, group, ns, kb, cb, root_rows, root_cols = sizes
    depth = cols // 2
    tb = ns // rows
    ra = ns // (rows * cols)
    sa = ns // leaves
    leaf = lax.axis_index("leaf")
    y = lax.axis_index("row")
    c = lax.axis_index("col")
    z = c // 2
    core = c % 2
    y_next, y_prev, y_far = (y + 1) % rows, (y + rows - 1) % rows, (y + 2) % rows
    sibling = c + 1 - 2 * core

    def copy(src, dst, ss, rs, target):
        return pltpu.make_async_remote_copy(
            src_ref=src, dst_ref=dst, send_sem=ss, recv_sem=rs, device_id=target, device_id_type=MESH
        )

    fetch = [pltpu.make_async_copy(w_hbm.at[h], w_ref.at[h], in_sem.at[h]) for h in range(group)]
    fetch_root = pltpu.make_async_copy(sig_hbm, sig_ref, in_sem.at[group])
    fetch[0].start()
    fetch_root.start()
    fetch[1].start()

    barrier = pltpu.get_barrier_semaphore()
    for target in ({"row": y_next}, {"row": y_prev}, {"col": sibling}):
        pl.semaphore_signal(barrier, inc=1, device_id=target, device_id_type=MESH)
    for d in range(1, leaves):
        pl.semaphore_signal(barrier, inc=1, device_id={"leaf": (leaf + d) % leaves}, device_id_type=MESH)

    @pl.when(z > 0)
    def _():
        pl.semaphore_signal(barrier, inc=1, device_id={"col": c - 2}, device_id_type=MESH)

    @pl.when(z < depth - 1)
    def _():
        pl.semaphore_signal(barrier, inc=1, device_id={"col": c + 2}, device_id_type=MESH)

    corner = jnp.logical_or(
        jnp.logical_and(y == 0, z == depth - 1), jnp.logical_and(y == rows - 1, z == 0)
    )

    @pl.when(corner)
    def _():
        for k in range(2):
            pl.semaphore_signal(barrier, inc=1, device_id={"row": z, "col": 2 * y + k}, device_id_type=MESH)

    def view(item, slot):
        if item < group:
            return ig.at[slot, item]
        return aa.at[item - group, pl.ds(pl.multiple_of(slot * ra, ra), ra), :]

    def z_copy(item, way, step):
        slot = c - 2 * (step - 1) if way == 0 else c + 2 * (step - 1)
        target = c + 2 if way == 0 else c - 2
        return copy(
            view(item, slot), view(item, slot),
            z_ss.at[item, way, step - 1], z_rs.at[item, way, step - 1], {"col": target},
        )

    def z_cut(item, way, step):
        return step == depth - 1 and ((item == 0 and way == 1) or (item == 1 and way == 0))

    def z_sends(item, way, step):
        if z_cut(item, way, step):
            return None
        if way == 0:
            cond, origin = jnp.logical_and(z < depth - 1, z >= step - 1), z - step + 1
        else:
            cond, origin = jnp.logical_and(z > 0, z + step - 1 <= depth - 1), z + step - 1
        return jnp.logical_and(cond, origin <= y) if item < group else cond

    def z_gets(item, way, step):
        if z_cut(item, way, step):
            return None
        cond, origin = (z >= step, z - step) if way == 0 else (z + step <= depth - 1, z + step)
        return jnp.logical_and(cond, origin <= y) if item < group else cond

    def when(cond, do):
        if cond is not None:
            pl.when(cond)(do)

    def has_own(item):
        return z <= y if item < group else z >= 0

    def b_copy(item, origin):
        slot = 2 * origin + core
        return copy(view(item, slot), view(item, slot), b_ss.at[item, origin], b_rs.at[item, origin], {"col": sibling})

    def b_landed(item, origin):
        slot = 2 * origin + 1 - core
        copy(
            view(item, slot), view(item, slot), b_ss.at[item, origin], b_rs.at[item, origin], {"col": sibling}
        ).wait_recv()

    def z_start(item, way, step):
        when(z_sends(item, way, step), lambda: z_copy(item, way, step).start())

    def z_own(item):
        z_start(item, 0, 1)
        z_start(item, 1, 1)
        when(has_own(item), lambda: b_copy(item, z).start())

    def z_relay(item, step):
        for way in range(2):
            def relay():
                origin = z - step if way == 0 else z + step
                slot = 2 * origin + core
                copy(
                    view(item, slot), view(item, slot),
                    z_ss.at[item, way, step - 1], z_rs.at[item, way, step - 1], {"col": sibling},
                ).wait_recv()
                if step < depth - 1:
                    z_start(item, way, step + 1)
                b_copy(item, origin).start()

            when(z_gets(item, way, step), relay)

    def z_last(item):
        for origin in range(depth):
            b_landed(item, origin)

    def z_sent(item):
        for way in range(2):
            for step in range(1, depth):
                when(z_sends(item, way, step), lambda: z_copy(item, way, step).wait_send())
                when(z_gets(item, way, step), lambda: b_copy(item, z - step if way == 0 else z + step).wait_send())
        when(has_own(item), lambda: b_copy(item, z).wait_send())

    def rs_copies(part, half, whole, ss, rs):
        right, left = {"row": y_next}, {"row": y_prev}
        plan = (
            (part(y_far, 0), half(0), right),
            (part(y_far, 1), half(1), left),
            (part(y_next, 1), whole(0, 1), right),
            (part(y_prev, 0), whole(1, 0), left),
            (part(y_next, 0), whole(0, 0), right),
            (part(y_prev, 1), whole(1, 1), left),
        )
        return [copy(src, dst, ss.at[k], rs.at[k], target) for k, (src, dst, target) in enumerate(plan)]

    def p_part(h):
        return lambda s, k: pp.at[h, pl.ds(pl.multiple_of(s * tb + k * (tb // 2), tb // 2), tb // 2), :]

    def p_rs_copies(h):
        return rs_copies(
            p_part(h), lambda k: ph.at[h, k],
            lambda w, k: pr.at[h, w, k], p_ss.at[h], p_rs.at[h],
        )

    def d_part(h):
        return lambda s, k: dp.at[h, 2 * s + k]

    def d_rs_copies(h):
        return rs_copies(
            d_part(h), lambda k: dh.at[h, k],
            lambda w, k: dr.at[h, w, k], d_ss.at[h], d_rs.at[h],
        )

    def rs_round1(copies):
        for k in range(4):
            copies[k].start()

    def rs_round2(copies, part, half):
        copies[0].wait_recv()
        mine = part(y_next, 0)
        mine[...] = mine[...] + half(0)[...]
        copies[4].start()
        copies[1].wait_recv()
        mine = part(y_prev, 1)
        mine[...] = mine[...] + half(1)[...]
        copies[5].start()

    def rs_arrived(copies):
        for k in range(2, 6):
            copies[k].wait_recv()

    def sent(copies):
        for one in copies:
            one.wait_send()

    def ag_copies(slot, ss, rs):
        right, left = {"row": y_next}, {"row": y_prev}
        plan = (
            (slot(y, 0), right), (slot(y, 1), left), (slot(y, 1), right), (slot(y, 0), left),
            (slot(y_prev, 0), right), (slot(y_next, 1), left),
        )
        return [copy(src, src, ss.at[k], rs.at[k], target) for k, (src, target) in enumerate(plan)]

    def pf_copies(h):
        slot = lambda s, k: pf.at[h, pl.ds(pl.multiple_of(s * tb + k * (tb // 2), tb // 2), tb // 2), :]
        return ag_copies(slot, a_ss.at[h], a_rs.at[h])

    def qt_copies(h):
        slot = lambda s, k: qt.at[h, s, pl.ds(k * (cb // 2), cb // 2), :]
        return ag_copies(slot, s_ss.at[h], s_rs.at[h])

    def ag_round1(copies):
        for k in range(4):
            copies[k].start()

    def ag_round2(copies):
        copies[0].wait_recv()
        copies[4].start()
        copies[1].wait_recv()
        copies[5].start()

    def ag_arrived(copies):
        for k in range(2, 6):
            copies[k].wait_recv()

    def product_partial(h):
        fetch[h].wait()

        @pl.loop(0, rows)
        def _(s):
            at = pl.ds(pl.multiple_of(s * tb, tb), tb)
            pp[h, at, :] = dot3(w_ref[h, at, :], i_ref[h])

    def pick():
        fetch_root.wait()
        place = y * cols + c
        share = pl.multiple_of((place * ra) // 128 * 128, 128)
        col_idx[...] = st_ref[:, pl.ds(share, min(128, ns))].T - place * root_cols
        mine = col_idx[pl.ds(pl.multiple_of(place * ra - share, ra), ra), :]
        at = pl.ds(pl.multiple_of(leaf * sa, sa), sa)
        lanes = lax.broadcasted_iota(jnp.int32, (ra, root_cols), 1)
        for h in range(leaves * group):
            row_idx[h] = st_ref[pl.ds(h, 1), at] - leaf * root_rows
            hot_col[pl.ds(h * ra, ra), :] = jnp.where(lanes == mine[:, h : h + 1], 1.0, 0.0).astype(BF16)
        high, low = split(sig_ref[...])
        chosen = hot_col[...]
        yt[0] = dot_t(chosen, high).astype(BF16)
        yt[1] = dot_t(chosen, low).astype(BF16)
        sublanes = lax.broadcasted_iota(jnp.int32, (root_rows, sa), 0)

        @pl.loop(0, leaves * group)
        def _(h):
            hot = jnp.where(sublanes == row_idx[h], 1.0, 0.0).astype(BF16)
            mine = pl.ds(pl.multiple_of(h * ra, ra), ra)
            both = dot(jnp.concatenate([yt[0, mine, :], yt[1, mine, :]], axis=0), hot)
            asend[h] = both[:ra] + both[ra:]

    def l_copies():
        out = []
        for d in range(1, leaves):
            target = (leaf + d) % leaves
            out.append(copy(
                asend.at[pl.ds(target * group, group)],
                aa.at[:, pl.ds(pl.multiple_of(c * ra, ra), ra), pl.ds(pl.multiple_of(leaf * sa, sa), sa)],
                l_ss.at[d - 1], l_rs.at[d - 1], {"leaf": target},
            ))
        return out

    def product_done(h):
        for k in range(2):
            at = pl.ds(pl.multiple_of(y * tb + k * (tb // 2), tb // 2), tb // 2)
            pf[h, at, :] = pp[h, at, :] + (pr[h, 0, k] + pr[h, 1, k])

    def ancestor_times(h):
        total = dot3(aa[h, :, pl.ds(0, tb)], pf[h, pl.ds(0, tb), :])
        for s in range(1, rows):
            total = total + dot3(aa[h, :, pl.ds(s * tb, tb)], pf[h, pl.ds(s * tb, tb), :])
        sp_ref[h] = -total
        qt[h, y] = total.T

    def right_terms(h):
        nt[h] = it[h] + dot3(qt[h, 0], w_ref[h, pl.ds(0, tb), :])

        @pl.loop(1, rows)
        def _(s):
            nt[h] = nt[h] + dot3(qt[h, s], w_ref[h, pl.ds(pl.multiple_of(s * tb, tb), tb), :])

    def uncut(h):
        return z < depth - 1 if h == 1 else z >= 0

    def d_goes(h):
        late = jnp.logical_or(y >= 2, jnp.logical_and(y == 1, uncut(h)))
        far = jnp.logical_or(y == 3, jnp.logical_and(y == 2, uncut(h)))
        wrap = jnp.logical_and(y == 3, uncut(h))
        return (far, far, wrap, late, jnp.logical_or(y == 0, wrap), late)

    def diagonal_slice(h, copies, origin):
        b_landed(h, origin)
        for k in range(2):
            dp[h, 2 * origin + k] = dot3(nt[h], ig[2 * origin + k, h])

        @pl.when(origin == y_far)
        def _():
            copies[0].start()
            copies[1].start()

        @pl.when(origin == y_next)
        def _():
            copies[2].start()

        @pl.when(origin == y_prev)
        def _():
            copies[3].start()

            @pl.when(y == 3)
            def _():
                copies[5].start()

    def diagonal_step(h, copies, step):
        if step == 0:
            when(z <= y, lambda: diagonal_slice(h, copies, z))
            return
        for way in range(2):
            when(z_gets(h, way, step), lambda: diagonal_slice(h, copies, z - step if way == 0 else z + step))

    def d_round2(h, copies):
        @pl.when(jnp.logical_and(y == 3, uncut(h)))
        def _():
            copies[0].wait_recv()
            dp[h, 0] = dp[h, 0] + dh[h, 0]
            copies[4].start()

        @pl.when(y == 0)
        def _():
            copies[0].wait_recv()
            dp[h, 2] = dh[h, 0]
            copies[4].start()

        @pl.when(jnp.logical_or(y == 2, jnp.logical_and(y == 1, uncut(h))))
        def _():
            copies[1].wait_recv()
            mine = d_part(h)(y_prev, 1)
            mine[...] = mine[...] + dh[h, 1]
            copies[5].start()

    def d_finish(h, copies):
        first = jnp.logical_and(y == 0, uncut(h))
        middle = jnp.logical_or(y == 1, y == 2)

        @pl.when(jnp.logical_or(first, middle))
        def _():
            copies[3].wait_recv()
            dp[h, 2 * y] = dp[h, 2 * y] + dr[h, 1, 0]

        @pl.when(jnp.logical_or(first, y == 1))
        def _():
            copies[4].wait_recv()
            dp[h, 2 * y] = dp[h, 2 * y] + dr[h, 0, 0]

        @pl.when(first)
        def _():
            copies[2].wait_recv()
            dp[h, 2 * y + 1] = dp[h, 2 * y + 1] + dr[h, 0, 1]

        @pl.when(jnp.logical_or(first, middle))
        def _():
            copies[5].wait_recv()
            dp[h, 2 * y + 1] = dp[h, 2 * y + 1] + dr[h, 1, 1]

        mirrored = jnp.logical_and(corner, (y == 3) if h == 0 else (y == 0))

        @pl.when(jnp.logical_not(mirrored))
        def _():
            for k in range(2):
                sd_ref[h, pl.ds(k * cb, cb), :] = dp[h, 2 * y + k].T

    def m_copy(h, k):
        return copy(dp.at[h, 2 * y + k], ml.at[core], m_ss.at[k], m_rs.at[core], {"row": z, "col": 2 * y + k})

    def m_sends(h):
        return jnp.logical_and(corner, (y == 0) if h == 0 else (y == 3))

    def m_start(h):
        @pl.when(m_sends(h))
        def _():
            for k in range(2):
                m_copy(h, k).start()

    def m_finish(h):
        @pl.when(jnp.logical_and(corner, (y == 3) if h == 0 else (y == 0)))
        def _():
            for k in range(2):
                copy(ml.at[k], ml.at[k], m_ss.at[k], m_rs.at[k], {"row": z}).wait_recv()
                sd_ref[h, pl.ds(k * cb, cb), :] = ml[k]

        @pl.when(m_sends(h))
        def _():
            for k in range(2):
                m_copy(h, k).wait_send()

    p0, p1 = p_rs_copies(0), p_rs_copies(1)
    f0, f1 = pf_copies(0), pf_copies(1)
    q0, q1 = qt_copies(0), qt_copies(1)
    d0, d1 = d_rs_copies(0), d_rs_copies(1)
    exchange = l_copies()

    ig[c] = i_ref[...]
    product_partial(0)
    pick()
    pl.semaphore_wait(barrier, 2 + leaves + (z > 0).astype(jnp.int32) + (z < depth - 1).astype(jnp.int32)
        + 2 * corner.astype(jnp.int32))
    for one in exchange:
        one.start()
    aa[:, pl.ds(pl.multiple_of(c * ra, ra), ra), pl.ds(pl.multiple_of(leaf * sa, sa), sa)] = asend[
        pl.ds(leaf * group, group)
    ]
    rs_round1(p0)
    z_own(0)
    rs_round2(p0, p_part(0), lambda k: ph.at[0, k])
    rs_arrived(p0)
    product_done(0)
    ag_round1(f0)
    product_partial(1)
    rs_round1(p1)
    for one in exchange:
        one.wait_recv()
    z_own(2)
    z_own(3)
    ag_round2(f0)
    z_relay(2, 1)
    z_relay(2, 2)
    rs_round2(p1, p_part(1), lambda k: ph.at[1, k])
    rs_arrived(p1)
    product_done(1)
    ag_round1(f1)
    z_relay(3, 1)
    z_relay(0, 1)
    z_relay(2, 3)
    ag_arrived(f0)
    z_last(2)
    ancestor_times(0)
    ag_round1(q0)
    ag_round2(f1)
    z_relay(3, 2)
    ag_round2(q0)
    for h in range(group):
        it[h] = i_ref[h].T
    z_relay(3, 3)
    ag_arrived(f1)
    z_last(3)
    ancestor_times(1)
    ag_round1(q1)
    z_relay(0, 2)
    z_own(1)
    ag_arrived(q0)
    right_terms(0)
    ag_round2(q1)
    diagonal_step(0, d0, 0)
    diagonal_step(0, d0, 1)
    z_relay(0, 3)
    diagonal_step(0, d0, 2)
    diagonal_step(0, d0, 3)
    ag_arrived(q1)
    right_terms(1)
    diagonal_step(1, d1, 0)
    d_round2(0, d0)
    z_relay(1, 1)
    diagonal_step(1, d1, 1)
    z_relay(1, 2)
    diagonal_step(1, d1, 2)
    d_finish(0, d0)
    m_start(0)
    z_relay(1, 3)
    diagonal_step(1, d1, 3)
    m_start(1)
    d_round2(1, d1)
    d_finish(1, d1)
    m_finish(0)
    m_finish(1)

    for copies in (p0, p1, f0, f1, q0, q1, exchange):
        sent(copies)
    for h, copies in enumerate((d0, d1)):
        for cond, one in zip(d_goes(h), copies):
            when(cond, one.wait_send)
    for item in range(2 * group):
        z_sent(item)


def hand_over(sp_in, sd_in, sp_out, sd_out):
    sp_out[...] = sp_in[...]
    sd_out[...] = sd_in[...]


def body(sigma_root, structure, inv_diag, panel):
    leaves, rows, cols = lax.axis_size("leaf"), lax.axis_size("row"), lax.axis_size("col")
    group, kb, cb = inv_diag.shape
    ns = panel.shape[1]
    children = structure.shape[0]
    root_rows, root_cols = sigma_root.shape
    ra = ns // (rows * cols)
    sa = ns // leaves
    tb = ns // rows
    dma = pltpu.SemaphoreType.DMA
    vmem = pltpu.VMEM
    items = 2 * group
    depth = cols // 2
    made = pl.pallas_call(
        partial(kernel, (leaves, rows, cols, group, ns, kb, cb, root_rows, root_cols)),
        out_shape=(
            jax.ShapeDtypeStruct((group, tb, cb), F32),
            jax.ShapeDtypeStruct((group, kb, cb), F32),
        ),
        in_specs=[pl.BlockSpec(memory_space=kind) for kind in (pl.ANY, vmem, pl.ANY, vmem)],
        out_specs=[pl.BlockSpec(memory_space=vmem)] * 2,
        scratch_shapes=[
            vmem(panel.shape, F32),
            vmem(sigma_root.shape, F32),
            vmem((cols, group, kb, cb), F32),
            vmem((group, tb, ns), F32),
            vmem((children, ra, sa), F32),
            vmem((children * ra, root_cols), BF16),
            vmem((min(128, ns), children), jnp.int32),
            vmem((children, 1, sa), jnp.int32),
            vmem((2, children * ra, root_rows), BF16),
            vmem((group, ns, cb), F32),
            vmem((group, 2, tb // 2, cb), F32),
            vmem((group, 2, 2, tb // 2, cb), F32),
            vmem((group, ns, cb), F32),
            vmem((group, rows, cb, tb), F32),
            vmem((group, cb, kb), F32),
            vmem((group, cb, kb), F32),
            vmem((group, cols, cb, cb), F32),
            vmem((group, 2, cb, cb), F32),
            vmem((group, 2, 2, cb, cb), F32),
            vmem((2, cb, cb), F32),
            dma((items, 2, depth - 1)), dma((items, 2, depth - 1)),
            dma((items, depth)), dma((items, depth)),
            dma((leaves - 1,)), dma((leaves - 1,)),
            dma((group, 6)), dma((group, 6)),
            dma((group, 6)), dma((group, 6)),
            dma((group, 6)), dma((group, 6)),
            dma((group, 6)), dma((group, 6)),
            dma((2,)), dma((2,)),
            dma((group + 1,)),
        ],
        compiler_params=pltpu.CompilerParams(
            collective_id=0, has_side_effects=True, vmem_limit_bytes=56 * 1024 * 1024
        ),
    )(panel, inv_diag, sigma_root, structure)
    return pl.pallas_call(
        hand_over, out_shape=tuple(jax.ShapeDtypeStruct(one.shape, one.dtype) for one in made)
    )(*made)


def solution(mesh):
    placed = (P("leaf", ("row", "col")), P(), P("leaf", "row", "col"), P("leaf", None, "row"))
    return jax.shard_map(
        body,
        mesh=mesh,
        in_specs=placed,
        out_specs=(P("leaf", "row", "col"), P("leaf", "row", "col")),
        check_vma=False,
    )
```

```python
from functools import partial

import jax
import jax.numpy as jnp
from jax import lax
from jax.experimental import pallas as pl
from jax.experimental.pallas import tpu as pltpu
from jax.sharding import PartitionSpec as P

MESH = pl.DeviceIdType.MESH
F32 = jnp.float32
BF16 = jnp.bfloat16


def split(x):
    high = x.astype(BF16)
    return high, (x - high.astype(F32)).astype(BF16)


def dot(a, b):
    return lax.dot_general(a, b, (((1,), (0,)), ((), ())), preferred_element_type=F32)


def dot_t(a, b):
    return lax.dot_general(a, b, (((1,), (1,)), ((), ())), preferred_element_type=F32)


def dot3(a, b):
    ah, al = split(a)
    bh, bl = split(b)
    return dot(ah, bh) + (dot(ah, bl) + dot(al, bh))


def kernel(
    sizes,
    w_hbm, i_ref, sig_hbm, st_ref,
    sp_ref, sd_ref,
    w_ref, sig_ref, ig, aa, asend, hot_col, col_idx, row_idx, yt, pp, ph, pr, pf, qt, it, nt, dp, dh, dr,
    ml, z_ss, z_rs, b_ss, b_rs, l_ss, l_rs, p_ss, p_rs, a_ss, a_rs, s_ss, s_rs, d_ss, d_rs, m_ss, m_rs, in_sem,
):
    leaves, rows, cols, group, ns, kb, cb, root_rows, root_cols = sizes
    depth = cols // 2
    tb = ns // rows
    ra = ns // (rows * cols)
    sa = ns // leaves
    leaf = lax.axis_index("leaf")
    y = lax.axis_index("row")
    c = lax.axis_index("col")
    z = c // 2
    core = c % 2
    y_next, y_prev, y_far = (y + 1) % rows, (y + rows - 1) % rows, (y + 2) % rows
    sibling = c + 1 - 2 * core

    def copy(src, dst, ss, rs, target):
        return pltpu.make_async_remote_copy(
            src_ref=src, dst_ref=dst, send_sem=ss, recv_sem=rs, device_id=target, device_id_type=MESH
        )

    fetch = [pltpu.make_async_copy(w_hbm.at[h], w_ref.at[h], in_sem.at[h]) for h in range(group)]
    fetch_root = pltpu.make_async_copy(sig_hbm, sig_ref, in_sem.at[group])
    fetch[0].start()
    fetch_root.start()
    fetch[1].start()

    barrier = pltpu.get_barrier_semaphore()
    for target in ({"row": y_next}, {"row": y_prev}, {"col": sibling}):
        pl.semaphore_signal(barrier, inc=1, device_id=target, device_id_type=MESH)
    for d in range(1, leaves):
        pl.semaphore_signal(barrier, inc=1, device_id={"leaf": (leaf + d) % leaves}, device_id_type=MESH)

    @pl.when(z > 0)
    def _():
        pl.semaphore_signal(barrier, inc=1, device_id={"col": c - 2}, device_id_type=MESH)

    @pl.when(z < depth - 1)
    def _():
        pl.semaphore_signal(barrier, inc=1, device_id={"col": c + 2}, device_id_type=MESH)

    corner = jnp.logical_or(
        jnp.logical_and(y == 0, z == depth - 1), jnp.logical_and(y == rows - 1, z == 0)
    )

    @pl.when(corner)
    def _():
        for k in range(2):
            pl.semaphore_signal(barrier, inc=1, device_id={"row": z, "col": 2 * y + k}, device_id_type=MESH)

    def view(item, slot):
        if item < group:
            return ig.at[slot, item]
        return aa.at[item - group, pl.ds(pl.multiple_of(slot * ra, ra), ra), :]

    def z_copy(item, way, step):
        slot = c - 2 * (step - 1) if way == 0 else c + 2 * (step - 1)
        target = c + 2 if way == 0 else c - 2
        return copy(
            view(item, slot), view(item, slot),
            z_ss.at[item, way, step - 1], z_rs.at[item, way, step - 1], {"col": target},
        )

    def z_cut(item, way, step):
        return step == depth - 1 and ((item == 0 and way == 1) or (item == 1 and way == 0))

    def z_sends(item, way, step):
        if z_cut(item, way, step):
            return None
        if way == 0:
            cond, origin = jnp.logical_and(z < depth - 1, z >= step - 1), z - step + 1
        else:
            cond, origin = jnp.logical_and(z > 0, z + step - 1 <= depth - 1), z + step - 1
        return jnp.logical_and(cond, origin <= y) if item < group else cond

    def z_gets(item, way, step):
        if z_cut(item, way, step):
            return None
        cond, origin = (z >= step, z - step) if way == 0 else (z + step <= depth - 1, z + step)
        return jnp.logical_and(cond, origin <= y) if item < group else cond

    def when(cond, do):
        if cond is not None:
            pl.when(cond)(do)

    def has_own(item):
        return z <= y if item < group else z >= 0

    def b_copy(item, origin):
        slot = 2 * origin + core
        return copy(view(item, slot), view(item, slot), b_ss.at[item, origin], b_rs.at[item, origin], {"col": sibling})

    def b_landed(item, origin):
        slot = 2 * origin + 1 - core
        copy(
            view(item, slot), view(item, slot), b_ss.at[item, origin], b_rs.at[item, origin], {"col": sibling}
        ).wait_recv()

    def z_start(item, way, step):
        when(z_sends(item, way, step), lambda: z_copy(item, way, step).start())

    def z_own(item):
        z_start(item, 0, 1)
        z_start(item, 1, 1)
        when(has_own(item), lambda: b_copy(item, z).start())

    def z_own_early(item):
        when(jnp.logical_and(z_sends(item, 0, 1), z < depth - 2), lambda: z_copy(item, 0, 1).start())
        z_start(item, 1, 1)
        when(has_own(item), lambda: b_copy(item, z).start())

    def z_own_late(item):
        when(jnp.logical_and(z_sends(item, 0, 1), z == depth - 2), lambda: z_copy(item, 0, 1).start())

    def z_relay(item, step):
        for way in range(2):
            def relay():
                origin = z - step if way == 0 else z + step
                slot = 2 * origin + core
                copy(
                    view(item, slot), view(item, slot),
                    z_ss.at[item, way, step - 1], z_rs.at[item, way, step - 1], {"col": sibling},
                ).wait_recv()
                if step < depth - 1:
                    z_start(item, way, step + 1)
                b_copy(item, origin).start()

            when(z_gets(item, way, step), relay)

    def z_last(item):
        for origin in range(depth):
            b_landed(item, origin)

    def z_sent(item):
        for way in range(2):
            for step in range(1, depth):
                when(z_sends(item, way, step), lambda: z_copy(item, way, step).wait_send())
                when(z_gets(item, way, step), lambda: b_copy(item, z - step if way == 0 else z + step).wait_send())
        when(has_own(item), lambda: b_copy(item, z).wait_send())

    def rs_copies(part, half, whole, ss, rs):
        right, left = {"row": y_next}, {"row": y_prev}
        plan = (
            (part(y_far, 0), half(0), right),
            (part(y_far, 1), half(1), left),
            (part(y_next, 1), whole(0, 1), right),
            (part(y_prev, 0), whole(1, 0), left),
            (part(y_next, 0), whole(0, 0), right),
            (part(y_prev, 1), whole(1, 1), left),
        )
        return [copy(src, dst, ss.at[k], rs.at[k], target) for k, (src, dst, target) in enumerate(plan)]

    def p_part(h):
        return lambda s, k: pp.at[h, pl.ds(pl.multiple_of(s * tb + k * (tb // 2), tb // 2), tb // 2), :]

    def p_rs_copies(h):
        return rs_copies(
            p_part(h), lambda k: ph.at[h, k],
            lambda w, k: pr.at[h, w, k], p_ss.at[h], p_rs.at[h],
        )

    def d_part(h):
        return lambda s, k: dp.at[h, 2 * s + k]

    def d_rs_copies(h):
        return rs_copies(
            d_part(h), lambda k: dh.at[h, k],
            lambda w, k: dr.at[h, w, k], d_ss.at[h], d_rs.at[h],
        )

    def rs_round1(copies):
        for k in range(4):
            copies[k].start()

    def rs_round2(copies, part, half):
        copies[0].wait_recv()
        mine = part(y_next, 0)
        mine[...] = mine[...] + half(0)[...]
        copies[4].start()
        copies[1].wait_recv()
        mine = part(y_prev, 1)
        mine[...] = mine[...] + half(1)[...]
        copies[5].start()

    def rs_arrived(copies):
        for k in range(2, 6):
            copies[k].wait_recv()

    def sent(copies):
        for one in copies:
            one.wait_send()

    def ag_copies(slot, ss, rs):
        right, left = {"row": y_next}, {"row": y_prev}
        plan = (
            (slot(y, 0), right), (slot(y, 1), left), (slot(y, 1), right), (slot(y, 0), left),
            (slot(y_prev, 0), right), (slot(y_next, 1), left),
        )
        return [copy(src, src, ss.at[k], rs.at[k], target) for k, (src, target) in enumerate(plan)]

    def pf_copies(h):
        slot = lambda s, k: pf.at[h, pl.ds(pl.multiple_of(s * tb + k * (tb // 2), tb // 2), tb // 2), :]
        return ag_copies(slot, a_ss.at[h], a_rs.at[h])

    def qt_copies(h):
        slot = lambda s, k: qt.at[h, s, pl.ds(k * (cb // 2), cb // 2), :]
        return ag_copies(slot, s_ss.at[h], s_rs.at[h])

    def ag_round1(copies):
        for k in range(4):
            copies[k].start()

    def ag_round2(copies):
        copies[0].wait_recv()
        copies[4].start()
        copies[1].wait_recv()
        copies[5].start()

    def ag_arrived(copies):
        for k in range(2, 6):
            copies[k].wait_recv()

    def product_partial(h):
        fetch[h].wait()

        @pl.loop(0, rows)
        def _(s):
            at = pl.ds(pl.multiple_of(s * tb, tb), tb)
            pp[h, at, :] = dot3(w_ref[h, at, :], i_ref[h])

    def pick():
        fetch_root.wait()
        place = y * cols + c
        share = pl.multiple_of((place * ra) // 128 * 128, 128)
        col_idx[...] = st_ref[:, pl.ds(share, min(128, ns))].T - place * root_cols
        mine = col_idx[pl.ds(pl.multiple_of(place * ra - share, ra), ra), :]
        at = pl.ds(pl.multiple_of(leaf * sa, sa), sa)
        lanes = lax.broadcasted_iota(jnp.int32, (ra, root_cols), 1)
        for h in range(leaves * group):
            row_idx[h] = st_ref[pl.ds(h, 1), at] - leaf * root_rows
            hot_col[pl.ds(h * ra, ra), :] = jnp.where(lanes == mine[:, h : h + 1], 1.0, 0.0).astype(BF16)
        high, low = split(sig_ref[...])
        chosen = hot_col[...]
        yt[0] = dot_t(chosen, high).astype(BF16)
        yt[1] = dot_t(chosen, low).astype(BF16)
        sublanes = lax.broadcasted_iota(jnp.int32, (root_rows, sa), 0)

        @pl.loop(0, leaves * group)
        def _(h):
            hot = jnp.where(sublanes == row_idx[h], 1.0, 0.0).astype(BF16)
            mine = pl.ds(pl.multiple_of(h * ra, ra), ra)
            both = dot(jnp.concatenate([yt[0, mine, :], yt[1, mine, :]], axis=0), hot)
            asend[h] = both[:ra] + both[ra:]

    def l_copies():
        out = []
        for d in range(1, leaves):
            target = (leaf + d) % leaves
            out.append(copy(
                asend.at[pl.ds(target * group, group)],
                aa.at[:, pl.ds(pl.multiple_of(c * ra, ra), ra), pl.ds(pl.multiple_of(leaf * sa, sa), sa)],
                l_ss.at[d - 1], l_rs.at[d - 1], {"leaf": target},
            ))
        return out

    def product_done(h):
        for k in range(2):
            at = pl.ds(pl.multiple_of(y * tb + k * (tb // 2), tb // 2), tb // 2)
            pf[h, at, :] = pp[h, at, :] + (pr[h, 0, k] + pr[h, 1, k])

    def ancestor_times(h):
        total = dot3(aa[h, :, pl.ds(0, tb)], pf[h, pl.ds(0, tb), :])
        for s in range(1, rows):
            total = total + dot3(aa[h, :, pl.ds(s * tb, tb)], pf[h, pl.ds(s * tb, tb), :])
        sp_ref[h] = -total
        qt[h, y] = total.T

    def right_terms(h):
        nt[h] = it[h] + dot3(qt[h, 0], w_ref[h, pl.ds(0, tb), :])

        @pl.loop(1, rows)
        def _(s):
            nt[h] = nt[h] + dot3(qt[h, s], w_ref[h, pl.ds(pl.multiple_of(s * tb, tb), tb), :])

    def uncut(h):
        return z < depth - 1 if h == 1 else z >= 0

    def d_goes(h):
        late = jnp.logical_or(y >= 2, jnp.logical_and(y == 1, uncut(h)))
        far = jnp.logical_or(y == 3, jnp.logical_and(y == 2, uncut(h)))
        wrap = jnp.logical_and(y == 3, uncut(h))
        return (far, far, wrap, late, jnp.logical_or(y == 0, wrap), late)

    def diagonal_slice(h, copies, origin):
        b_landed(h, origin)
        for k in range(2):
            dp[h, 2 * origin + k] = dot3(nt[h], ig[2 * origin + k, h])

        @pl.when(origin == y_far)
        def _():
            copies[0].start()
            copies[1].start()

        @pl.when(origin == y_next)
        def _():
            copies[2].start()

        @pl.when(origin == y_prev)
        def _():
            copies[3].start()

            @pl.when(y == 3)
            def _():
                copies[5].start()

    def diagonal_step(h, copies, step):
        if step == 0:
            when(z <= y, lambda: diagonal_slice(h, copies, z))
            return
        for way in range(2):
            when(z_gets(h, way, step), lambda: diagonal_slice(h, copies, z - step if way == 0 else z + step))

    def d_round2(h, copies):
        @pl.when(jnp.logical_and(y == 3, uncut(h)))
        def _():
            copies[0].wait_recv()
            dp[h, 0] = dp[h, 0] + dh[h, 0]
            copies[4].start()

        @pl.when(y == 0)
        def _():
            copies[0].wait_recv()
            dp[h, 2] = dh[h, 0]
            copies[4].start()

        @pl.when(jnp.logical_or(y == 2, jnp.logical_and(y == 1, uncut(h))))
        def _():
            copies[1].wait_recv()
            mine = d_part(h)(y_prev, 1)
            mine[...] = mine[...] + dh[h, 1]
            copies[5].start()

    def d_finish(h, copies):
        first = jnp.logical_and(y == 0, uncut(h))
        middle = jnp.logical_or(y == 1, y == 2)

        @pl.when(jnp.logical_or(first, middle))
        def _():
            copies[3].wait_recv()
            dp[h, 2 * y] = dp[h, 2 * y] + dr[h, 1, 0]

        @pl.when(jnp.logical_or(first, y == 1))
        def _():
            copies[4].wait_recv()
            dp[h, 2 * y] = dp[h, 2 * y] + dr[h, 0, 0]

        @pl.when(first)
        def _():
            copies[2].wait_recv()
            dp[h, 2 * y + 1] = dp[h, 2 * y + 1] + dr[h, 0, 1]

        @pl.when(jnp.logical_or(first, middle))
        def _():
            copies[5].wait_recv()
            dp[h, 2 * y + 1] = dp[h, 2 * y + 1] + dr[h, 1, 1]

        mirrored = jnp.logical_and(corner, (y == 3) if h == 0 else (y == 0))

        @pl.when(jnp.logical_not(mirrored))
        def _():
            for k in range(2):
                sd_ref[h, pl.ds(k * cb, cb), :] = dp[h, 2 * y + k].T

    def m_copy(h, k):
        return copy(dp.at[h, 2 * y + k], ml.at[core], m_ss.at[k], m_rs.at[core], {"row": z, "col": 2 * y + k})

    def m_sends(h):
        return jnp.logical_and(corner, (y == 0) if h == 0 else (y == 3))

    def m_start(h):
        @pl.when(m_sends(h))
        def _():
            for k in range(2):
                m_copy(h, k).start()

    def m_finish(h):
        @pl.when(jnp.logical_and(corner, (y == 3) if h == 0 else (y == 0)))
        def _():
            for k in range(2):
                copy(ml.at[k], ml.at[k], m_ss.at[k], m_rs.at[k], {"row": z}).wait_recv()
                sd_ref[h, pl.ds(k * cb, cb), :] = ml[k]

        @pl.when(m_sends(h))
        def _():
            for k in range(2):
                m_copy(h, k).wait_send()

    p0, p1 = p_rs_copies(0), p_rs_copies(1)
    f0, f1 = pf_copies(0), pf_copies(1)
    q0, q1 = qt_copies(0), qt_copies(1)
    d0, d1 = d_rs_copies(0), d_rs_copies(1)
    exchange = l_copies()

    ig[c] = i_ref[...]
    product_partial(0)
    pick()
    pl.semaphore_wait(barrier, 2 + leaves + (z > 0).astype(jnp.int32) + (z < depth - 1).astype(jnp.int32)
        + 2 * corner.astype(jnp.int32))
    for one in exchange:
        one.start()
    aa[:, pl.ds(pl.multiple_of(c * ra, ra), ra), pl.ds(pl.multiple_of(leaf * sa, sa), sa)] = asend[
        pl.ds(leaf * group, group)
    ]
    rs_round1(p0)
    z_own(0)
    rs_round2(p0, p_part(0), lambda k: ph.at[0, k])
    rs_arrived(p0)
    product_done(0)
    ag_round1(f0)
    product_partial(1)
    rs_round1(p1)
    for one in exchange:
        one.wait_recv()
    z_own(2)
    z_own(3)
    ag_round2(f0)
    z_relay(2, 1)
    z_relay(2, 2)
    rs_round2(p1, p_part(1), lambda k: ph.at[1, k])
    rs_arrived(p1)
    product_done(1)
    ag_round1(f1)
    z_relay(3, 1)
    z_relay(0, 1)
    z_relay(2, 3)
    ag_arrived(f0)
    z_last(2)
    ancestor_times(0)
    ag_round1(q0)
    ag_round2(f1)
    z_relay(3, 2)
    z_own_early(1)
    ag_round2(q0)
    for h in range(group):
        it[h] = i_ref[h].T
    z_relay(3, 3)
    ag_arrived(f1)
    z_last(3)
    ancestor_times(1)
    ag_round1(q1)
    z_relay(0, 2)
    z_own_late(1)
    ag_arrived(q0)
    right_terms(0)
    ag_round2(q1)
    diagonal_step(0, d0, 0)
    diagonal_step(0, d0, 1)
    z_relay(0, 3)
    diagonal_step(0, d0, 2)
    diagonal_step(0, d0, 3)
    ag_arrived(q1)
    right_terms(1)
    diagonal_step(1, d1, 0)
    d_round2(0, d0)
    z_relay(1, 1)
    diagonal_step(1, d1, 1)
    z_relay(1, 2)
    diagonal_step(1, d1, 2)
    d_finish(0, d0)
    m_start(0)
    z_relay(1, 3)
    diagonal_step(1, d1, 3)
    m_start(1)
    d_round2(1, d1)
    d_finish(1, d1)
    m_finish(0)
    m_finish(1)

    for copies in (p0, p1, f0, f1, q0, q1, exchange):
        sent(copies)
    for h, copies in enumerate((d0, d1)):
        for cond, one in zip(d_goes(h), copies):
            when(cond, one.wait_send)
    for item in range(2 * group):
        z_sent(item)


def hand_over(sp_in, sd_in, sp_out, sd_out):
    sp_out[...] = sp_in[...]
    sd_out[...] = sd_in[...]


def body(sigma_root, structure, inv_diag, panel):
    leaves, rows, cols = lax.axis_size("leaf"), lax.axis_size("row"), lax.axis_size("col")
    group, kb, cb = inv_diag.shape
    ns = panel.shape[1]
    children = structure.shape[0]
    root_rows, root_cols = sigma_root.shape
    ra = ns // (rows * cols)
    sa = ns // leaves
    tb = ns // rows
    dma = pltpu.SemaphoreType.DMA
    vmem = pltpu.VMEM
    items = 2 * group
    depth = cols // 2
    made = pl.pallas_call(
        partial(kernel, (leaves, rows, cols, group, ns, kb, cb, root_rows, root_cols)),
        out_shape=(
            jax.ShapeDtypeStruct((group, tb, cb), F32),
            jax.ShapeDtypeStruct((group, kb, cb), F32),
        ),
        in_specs=[pl.BlockSpec(memory_space=kind) for kind in (pl.ANY, vmem, pl.ANY, vmem)],
        out_specs=[pl.BlockSpec(memory_space=vmem)] * 2,
        scratch_shapes=[
            vmem(panel.shape, F32),
            vmem(sigma_root.shape, F32),
            vmem((cols, group, kb, cb), F32),
            vmem((group, tb, ns), F32),
            vmem((children, ra, sa), F32),
            vmem((children * ra, root_cols), BF16),
            vmem((min(128, ns), children), jnp.int32),
            vmem((children, 1, sa), jnp.int32),
            vmem((2, children * ra, root_rows), BF16),
            vmem((group, ns, cb), F32),
            vmem((group, 2, tb // 2, cb), F32),
            vmem((group, 2, 2, tb // 2, cb), F32),
            vmem((group, ns, cb), F32),
            vmem((group, rows, cb, tb), F32),
            vmem((group, cb, kb), F32),
            vmem((group, cb, kb), F32),
            vmem((group, cols, cb, cb), F32),
            vmem((group, 2, cb, cb), F32),
            vmem((group, 2, 2, cb, cb), F32),
            vmem((2, cb, cb), F32),
            dma((items, 2, depth - 1)), dma((items, 2, depth - 1)),
            dma((items, depth)), dma((items, depth)),
            dma((leaves - 1,)), dma((leaves - 1,)),
            dma((group, 6)), dma((group, 6)),
            dma((group, 6)), dma((group, 6)),
            dma((group, 6)), dma((group, 6)),
            dma((group, 6)), dma((group, 6)),
            dma((2,)), dma((2,)),
            dma((group + 1,)),
        ],
        compiler_params=pltpu.CompilerParams(
            collective_id=0, has_side_effects=True, vmem_limit_bytes=56 * 1024 * 1024
        ),
    )(panel, inv_diag, sigma_root, structure)
    return pl.pallas_call(
        hand_over, out_shape=tuple(jax.ShapeDtypeStruct(one.shape, one.dtype) for one in made)
    )(*made)


def solution(mesh):
    placed = (P("leaf", ("row", "col")), P(), P("leaf", "row", "col"), P("leaf", None, "row"))
    return jax.shard_map(
        body,
        mesh=mesh,
        in_specs=placed,
        out_specs=(P("leaf", "row", "col"), P("leaf", "row", "col")),
        check_vma=False,
    )
```

```python
from functools import partial

import jax
import jax.numpy as jnp
from jax import lax
from jax.experimental import pallas as pl
from jax.experimental.pallas import tpu as pltpu
from jax.sharding import PartitionSpec as P

MESH = pl.DeviceIdType.MESH
F32 = jnp.float32
BF16 = jnp.bfloat16


def split(x):
    high = x.astype(BF16)
    return high, (x - high.astype(F32)).astype(BF16)


def dot(a, b):
    return lax.dot_general(a, b, (((1,), (0,)), ((), ())), preferred_element_type=F32)


def dot_t(a, b):
    return lax.dot_general(a, b, (((1,), (1,)), ((), ())), preferred_element_type=F32)


def dot3(a, b):
    ah, al = split(a)
    bh, bl = split(b)
    return dot(ah, bh) + (dot(ah, bl) + dot(al, bh))


def kernel(
    sizes,
    w_hbm, i_ref, sig_hbm, st_ref,
    sp_ref, sd_ref,
    w_ref, sig_ref, ig, aa, asend, hot_col, col_idx, row_idx, yt, pp, ph, pr, pf, qt, it, nt, dp, dh, dr,
    ml, z_ss, z_rs, b_ss, b_rs, l_ss, l_rs, p_ss, p_rs, a_ss, a_rs, s_ss, s_rs, d_ss, d_rs, m_ss, m_rs, in_sem,
):
    leaves, rows, cols, group, ns, kb, cb, root_rows, root_cols = sizes
    depth = cols // 2
    tb = ns // rows
    ra = ns // (rows * cols)
    sa = ns // leaves
    leaf = lax.axis_index("leaf")
    y = lax.axis_index("row")
    c = lax.axis_index("col")
    z = c // 2
    core = c % 2
    y_next, y_prev, y_far = (y + 1) % rows, (y + rows - 1) % rows, (y + 2) % rows
    sibling = c + 1 - 2 * core

    def copy(src, dst, ss, rs, target):
        return pltpu.make_async_remote_copy(
            src_ref=src, dst_ref=dst, send_sem=ss, recv_sem=rs, device_id=target, device_id_type=MESH
        )

    fetch = [pltpu.make_async_copy(w_hbm.at[h], w_ref.at[h], in_sem.at[h]) for h in range(group)]
    fetch_root = pltpu.make_async_copy(sig_hbm, sig_ref, in_sem.at[group])
    fetch[0].start()
    fetch_root.start()
    fetch[1].start()

    barrier = pltpu.get_barrier_semaphore()
    for target in ({"row": y_next}, {"row": y_prev}, {"col": sibling}):
        pl.semaphore_signal(barrier, inc=1, device_id=target, device_id_type=MESH)
    for d in range(1, leaves):
        pl.semaphore_signal(barrier, inc=1, device_id={"leaf": (leaf + d) % leaves}, device_id_type=MESH)

    @pl.when(z > 0)
    def _():
        pl.semaphore_signal(barrier, inc=1, device_id={"col": c - 2}, device_id_type=MESH)

    @pl.when(z < depth - 1)
    def _():
        pl.semaphore_signal(barrier, inc=1, device_id={"col": c + 2}, device_id_type=MESH)

    corner = jnp.logical_or(
        jnp.logical_and(y == 0, z == depth - 1), jnp.logical_and(y == rows - 1, z == 0)
    )

    @pl.when(corner)
    def _():
        for k in range(2):
            pl.semaphore_signal(barrier, inc=1, device_id={"row": z, "col": 2 * y + k}, device_id_type=MESH)

    def view(item, slot):
        if item < group:
            return ig.at[slot, item]
        return aa.at[item - group, pl.ds(pl.multiple_of(slot * ra, ra), ra), :]

    def z_copy(item, way, step):
        slot = c - 2 * (step - 1) if way == 0 else c + 2 * (step - 1)
        target = c + 2 if way == 0 else c - 2
        return copy(
            view(item, slot), view(item, slot),
            z_ss.at[item, way, step - 1], z_rs.at[item, way, step - 1], {"col": target},
        )

    def z_cut(item, way, step):
        return step == depth - 1 and ((item == 0 and way == 1) or (item == 1 and way == 0))

    def z_sends(item, way, step):
        if z_cut(item, way, step):
            return None
        if way == 0:
            cond, origin = jnp.logical_and(z < depth - 1, z >= step - 1), z - step + 1
        else:
            cond, origin = jnp.logical_and(z > 0, z + step - 1 <= depth - 1), z + step - 1
        return jnp.logical_and(cond, origin <= y) if item < group else cond

    def z_gets(item, way, step):
        if z_cut(item, way, step):
            return None
        cond, origin = (z >= step, z - step) if way == 0 else (z + step <= depth - 1, z + step)
        return jnp.logical_and(cond, origin <= y) if item < group else cond

    def when(cond, do):
        if cond is not None:
            pl.when(cond)(do)

    def has_own(item):
        return z <= y if item < group else z >= 0

    def b_copy(item, origin):
        slot = 2 * origin + core
        return copy(view(item, slot), view(item, slot), b_ss.at[item, origin], b_rs.at[item, origin], {"col": sibling})

    def b_landed(item, origin):
        slot = 2 * origin + 1 - core
        copy(
            view(item, slot), view(item, slot), b_ss.at[item, origin], b_rs.at[item, origin], {"col": sibling}
        ).wait_recv()

    def z_start(item, way, step):
        when(z_sends(item, way, step), lambda: z_copy(item, way, step).start())

    def z_own(item):
        z_start(item, 0, 1)
        z_start(item, 1, 1)
        when(has_own(item), lambda: b_copy(item, z).start())

    def z_relay(item, step):
        for way in range(2):
            def relay():
                origin = z - step if way == 0 else z + step
                slot = 2 * origin + core
                copy(
                    view(item, slot), view(item, slot),
                    z_ss.at[item, way, step - 1], z_rs.at[item, way, step - 1], {"col": sibling},
                ).wait_recv()
                if step < depth - 1:
                    z_start(item, way, step + 1)
                b_copy(item, origin).start()

            when(z_gets(item, way, step), relay)

    def z_last(item):
        for origin in range(depth):
            b_landed(item, origin)

    def z_sent(item):
        for way in range(2):
            for step in range(1, depth):
                when(z_sends(item, way, step), lambda: z_copy(item, way, step).wait_send())
                when(z_gets(item, way, step), lambda: b_copy(item, z - step if way == 0 else z + step).wait_send())
        when(has_own(item), lambda: b_copy(item, z).wait_send())

    def rs_copies(part, half, whole, ss, rs):
        right, left = {"row": y_next}, {"row": y_prev}
        plan = (
            (part(y_far, 0), half(0), right),
            (part(y_far, 1), half(1), left),
            (part(y_next, 1), whole(0, 1), right),
            (part(y_prev, 0), whole(1, 0), left),
            (part(y_next, 0), whole(0, 0), right),
            (part(y_prev, 1), whole(1, 1), left),
        )
        return [copy(src, dst, ss.at[k], rs.at[k], target) for k, (src, dst, target) in enumerate(plan)]

    def p_part(h):
        return lambda s, k: pp.at[h, pl.ds(pl.multiple_of(s * tb + k * (tb // 2), tb // 2), tb // 2), :]

    def p_rs_copies(h):
        return rs_copies(
            p_part(h), lambda k: ph.at[h, k],
            lambda w, k: pr.at[h, w, k], p_ss.at[h], p_rs.at[h],
        )

    def d_part(h):
        return lambda s, k: dp.at[h, 2 * s + k]

    def d_rs_copies(h):
        return rs_copies(
            d_part(h), lambda k: dh.at[h, k],
            lambda w, k: dr.at[h, w, k], d_ss.at[h], d_rs.at[h],
        )

    def rs_round1(copies):
        for k in range(4):
            copies[k].start()

    def rs_round2(copies, part, half):
        copies[0].wait_recv()
        mine = part(y_next, 0)
        mine[...] = mine[...] + half(0)[...]
        copies[4].start()
        copies[1].wait_recv()
        mine = part(y_prev, 1)
        mine[...] = mine[...] + half(1)[...]
        copies[5].start()

    def rs_arrived(copies):
        for k in range(2, 6):
            copies[k].wait_recv()

    def sent(copies):
        for one in copies:
            one.wait_send()

    def ag_copies(slot, ss, rs):
        right, left = {"row": y_next}, {"row": y_prev}
        plan = (
            (slot(y, 0), right), (slot(y, 1), left), (slot(y, 1), right), (slot(y, 0), left),
            (slot(y_prev, 0), right), (slot(y_next, 1), left),
        )
        return [copy(src, src, ss.at[k], rs.at[k], target) for k, (src, target) in enumerate(plan)]

    def pf_copies(h):
        slot = lambda s, k: pf.at[h, pl.ds(pl.multiple_of(s * tb + k * (tb // 2), tb // 2), tb // 2), :]
        return ag_copies(slot, a_ss.at[h], a_rs.at[h])

    def qt_copies(h):
        slot = lambda s, k: qt.at[h, s, pl.ds(k * (cb // 2), cb // 2), :]
        return ag_copies(slot, s_ss.at[h], s_rs.at[h])

    def ag_round1(copies):
        for k in range(4):
            copies[k].start()

    def ag_round2(copies):
        copies[0].wait_recv()
        copies[4].start()
        copies[1].wait_recv()
        copies[5].start()

    def ag_arrived(copies):
        for k in range(2, 6):
            copies[k].wait_recv()

    def product_partial(h):
        fetch[h].wait()

        @pl.loop(0, rows)
        def _(s):
            at = pl.ds(pl.multiple_of(s * tb, tb), tb)
            pp[h, at, :] = dot3(w_ref[h, at, :], i_ref[h])

    def pick():
        fetch_root.wait()
        place = y * cols + c
        share = pl.multiple_of((place * ra) // 128 * 128, 128)
        col_idx[...] = st_ref[:, pl.ds(share, min(128, ns))].T - place * root_cols
        mine = col_idx[pl.ds(pl.multiple_of(place * ra - share, ra), ra), :]
        at = pl.ds(pl.multiple_of(leaf * sa, sa), sa)
        lanes = lax.broadcasted_iota(jnp.int32, (ra, root_cols), 1)
        for h in range(leaves * group):
            row_idx[h] = st_ref[pl.ds(h, 1), at] - leaf * root_rows
            hot_col[pl.ds(h * ra, ra), :] = jnp.where(lanes == mine[:, h : h + 1], 1.0, 0.0).astype(BF16)
        high, low = split(sig_ref[...])
        chosen = hot_col[...]
        yt[0] = dot_t(chosen, high).astype(BF16)
        yt[1] = dot_t(chosen, low).astype(BF16)
        sublanes = lax.broadcasted_iota(jnp.int32, (root_rows, sa), 0)

        @pl.loop(0, leaves * group)
        def _(h):
            hot = jnp.where(sublanes == row_idx[h], 1.0, 0.0).astype(BF16)
            mine = pl.ds(pl.multiple_of(h * ra, ra), ra)
            both = dot(jnp.concatenate([yt[0, mine, :], yt[1, mine, :]], axis=0), hot)
            asend[h] = both[:ra] + both[ra:]

    def l_copies():
        out = []
        for d in range(1, leaves):
            target = (leaf + d) % leaves
            out.append(copy(
                asend.at[pl.ds(target * group, group)],
                aa.at[:, pl.ds(pl.multiple_of(c * ra, ra), ra), pl.ds(pl.multiple_of(leaf * sa, sa), sa)],
                l_ss.at[d - 1], l_rs.at[d - 1], {"leaf": target},
            ))
        return out

    def product_done(h):
        for k in range(2):
            at = pl.ds(pl.multiple_of(y * tb + k * (tb // 2), tb // 2), tb // 2)
            pf[h, at, :] = pp[h, at, :] + (pr[h, 0, k] + pr[h, 1, k])

    def ancestor_times(h):
        total = dot3(aa[h, :, pl.ds(0, tb)], pf[h, pl.ds(0, tb), :])
        for s in range(1, rows):
            total = total + dot3(aa[h, :, pl.ds(s * tb, tb)], pf[h, pl.ds(s * tb, tb), :])
        sp_ref[h] = -total
        qt[h, y] = total.T

    def right_terms(h):
        nt[h] = it[h] + dot3(qt[h, 0], w_ref[h, pl.ds(0, tb), :])

        @pl.loop(1, rows)
        def _(s):
            nt[h] = nt[h] + dot3(qt[h, s], w_ref[h, pl.ds(pl.multiple_of(s * tb, tb), tb), :])

    def uncut(h):
        return z < depth - 1 if h == 1 else z >= 0

    def d_goes(h):
        late = jnp.logical_or(y >= 2, jnp.logical_and(y == 1, uncut(h)))
        far = jnp.logical_or(y == 3, jnp.logical_and(y == 2, uncut(h)))
        wrap = jnp.logical_and(y == 3, uncut(h))
        return (far, far, wrap, late, jnp.logical_or(y == 0, wrap), late)

    def diagonal_slice(h, copies, origin):
        b_landed(h, origin)
        for k in range(2):
            dp[h, 2 * origin + k] = dot3(nt[h], ig[2 * origin + k, h])

        @pl.when(origin == y_far)
        def _():
            copies[0].start()
            copies[1].start()

        @pl.when(origin == y_next)
        def _():
            copies[2].start()

        @pl.when(origin == y_prev)
        def _():
            copies[3].start()

            @pl.when(y == 3)
            def _():
                copies[5].start()

    def diagonal_step(h, copies, step):
        if step == 0:
            when(z <= y, lambda: diagonal_slice(h, copies, z))
            return
        for way in range(2):
            when(z_gets(h, way, step), lambda: diagonal_slice(h, copies, z - step if way == 0 else z + step))

    def d_round2(h, copies):
        @pl.when(jnp.logical_and(y == 3, uncut(h)))
        def _():
            copies[0].wait_recv()
            dp[h, 0] = dp[h, 0] + dh[h, 0]
            copies[4].start()

        @pl.when(y == 0)
        def _():
            copies[0].wait_recv()
            dp[h, 2] = dh[h, 0]
            copies[4].start()

        @pl.when(jnp.logical_or(y == 2, jnp.logical_and(y == 1, uncut(h))))
        def _():
            copies[1].wait_recv()
            mine = d_part(h)(y_prev, 1)
            mine[...] = mine[...] + dh[h, 1]
            copies[5].start()

    def d_finish(h, copies):
        first = jnp.logical_and(y == 0, uncut(h))
        middle = jnp.logical_or(y == 1, y == 2)

        @pl.when(jnp.logical_or(first, middle))
        def _():
            copies[3].wait_recv()
            dp[h, 2 * y] = dp[h, 2 * y] + dr[h, 1, 0]

        @pl.when(jnp.logical_or(first, y == 1))
        def _():
            copies[4].wait_recv()
            dp[h, 2 * y] = dp[h, 2 * y] + dr[h, 0, 0]

        @pl.when(first)
        def _():
            copies[2].wait_recv()
            dp[h, 2 * y + 1] = dp[h, 2 * y + 1] + dr[h, 0, 1]

        @pl.when(jnp.logical_or(first, middle))
        def _():
            copies[5].wait_recv()
            dp[h, 2 * y + 1] = dp[h, 2 * y + 1] + dr[h, 1, 1]

        mirrored = jnp.logical_and(corner, (y == 3) if h == 0 else (y == 0))

        @pl.when(jnp.logical_not(mirrored))
        def _():
            for k in range(2):
                sd_ref[h, pl.ds(k * cb, cb), :] = dp[h, 2 * y + k].T

    def m_copy(h, k):
        return copy(dp.at[h, 2 * y + k], ml.at[core], m_ss.at[k], m_rs.at[core], {"row": z, "col": 2 * y + k})

    def m_sends(h):
        return jnp.logical_and(corner, (y == 0) if h == 0 else (y == 3))

    def m_start(h):
        @pl.when(m_sends(h))
        def _():
            for k in range(2):
                m_copy(h, k).start()

    def m_finish(h):
        @pl.when(jnp.logical_and(corner, (y == 3) if h == 0 else (y == 0)))
        def _():
            for k in range(2):
                copy(ml.at[k], ml.at[k], m_ss.at[k], m_rs.at[k], {"row": z}).wait_recv()
                sd_ref[h, pl.ds(k * cb, cb), :] = ml[k]

        @pl.when(m_sends(h))
        def _():
            for k in range(2):
                m_copy(h, k).wait_send()

    p0, p1 = p_rs_copies(0), p_rs_copies(1)
    f0, f1 = pf_copies(0), pf_copies(1)
    q0, q1 = qt_copies(0), qt_copies(1)
    d0, d1 = d_rs_copies(0), d_rs_copies(1)
    exchange = l_copies()

    ig[c] = i_ref[...]
    product_partial(0)
    pick()
    product_partial(1)
    for h in range(group):
        it[h] = i_ref[h].T
    pl.semaphore_wait(barrier, 2 + leaves + (z > 0).astype(jnp.int32) + (z < depth - 1).astype(jnp.int32)
        + 2 * corner.astype(jnp.int32))
    for one in exchange:
        one.start()
    aa[:, pl.ds(pl.multiple_of(c * ra, ra), ra), pl.ds(pl.multiple_of(leaf * sa, sa), sa)] = asend[
        pl.ds(leaf * group, group)
    ]
    rs_round1(p0)
    z_own(0)
    rs_round2(p0, p_part(0), lambda k: ph.at[0, k])
    rs_arrived(p0)
    product_done(0)
    ag_round1(f0)
    rs_round1(p1)
    for one in exchange:
        one.wait_recv()
    z_own(2)
    z_own(3)
    ag_round2(f0)
    z_relay(2, 1)
    z_relay(2, 2)
    rs_round2(p1, p_part(1), lambda k: ph.at[1, k])
    rs_arrived(p1)
    product_done(1)
    ag_round1(f1)
    z_relay(3, 1)
    z_relay(0, 1)
    z_relay(2, 3)
    ag_arrived(f0)
    z_last(2)
    ancestor_times(0)
    ag_round1(q0)
    ag_round2(f1)
    z_relay(3, 2)
    ag_round2(q0)
    z_relay(3, 3)
    ag_arrived(f1)
    z_last(3)
    ancestor_times(1)
    ag_round1(q1)
    z_relay(0, 2)
    z_own(1)
    ag_arrived(q0)
    right_terms(0)
    ag_round2(q1)
    diagonal_step(0, d0, 0)
    diagonal_step(0, d0, 1)
    z_relay(0, 3)
    diagonal_step(0, d0, 2)
    diagonal_step(0, d0, 3)
    ag_arrived(q1)
    right_terms(1)
    diagonal_step(1, d1, 0)
    d_round2(0, d0)
    z_relay(1, 1)
    diagonal_step(1, d1, 1)
    z_relay(1, 2)
    diagonal_step(1, d1, 2)
    d_finish(0, d0)
    m_start(0)
    z_relay(1, 3)
    diagonal_step(1, d1, 3)
    m_start(1)
    d_round2(1, d1)
    d_finish(1, d1)
    m_finish(0)
    m_finish(1)

    for copies in (p0, p1, f0, f1, q0, q1, exchange):
        sent(copies)
    for h, copies in enumerate((d0, d1)):
        for cond, one in zip(d_goes(h), copies):
            when(cond, one.wait_send)
    for item in range(2 * group):
        z_sent(item)


def hand_over(sp_in, sd_in, sp_out, sd_out):
    sp_out[...] = sp_in[...]
    sd_out[...] = sd_in[...]


def body(sigma_root, structure, inv_diag, panel):
    leaves, rows, cols = lax.axis_size("leaf"), lax.axis_size("row"), lax.axis_size("col")
    group, kb, cb = inv_diag.shape
    ns = panel.shape[1]
    children = structure.shape[0]
    root_rows, root_cols = sigma_root.shape
    ra = ns // (rows * cols)
    sa = ns // leaves
    tb = ns // rows
    dma = pltpu.SemaphoreType.DMA
    vmem = pltpu.VMEM
    items = 2 * group
    depth = cols // 2
    made = pl.pallas_call(
        partial(kernel, (leaves, rows, cols, group, ns, kb, cb, root_rows, root_cols)),
        out_shape=(
            jax.ShapeDtypeStruct((group, tb, cb), F32),
            jax.ShapeDtypeStruct((group, kb, cb), F32),
        ),
        in_specs=[pl.BlockSpec(memory_space=kind) for kind in (pl.ANY, vmem, pl.ANY, vmem)],
        out_specs=[pl.BlockSpec(memory_space=vmem)] * 2,
        scratch_shapes=[
            vmem(panel.shape, F32),
            vmem(sigma_root.shape, F32),
            vmem((cols, group, kb, cb), F32),
            vmem((group, tb, ns), F32),
            vmem((children, ra, sa), F32),
            vmem((children * ra, root_cols), BF16),
            vmem((min(128, ns), children), jnp.int32),
            vmem((children, 1, sa), jnp.int32),
            vmem((2, children * ra, root_rows), BF16),
            vmem((group, ns, cb), F32),
            vmem((group, 2, tb // 2, cb), F32),
            vmem((group, 2, 2, tb // 2, cb), F32),
            vmem((group, ns, cb), F32),
            vmem((group, rows, cb, tb), F32),
            vmem((group, cb, kb), F32),
            vmem((group, cb, kb), F32),
            vmem((group, cols, cb, cb), F32),
            vmem((group, 2, cb, cb), F32),
            vmem((group, 2, 2, cb, cb), F32),
            vmem((2, cb, cb), F32),
            dma((items, 2, depth - 1)), dma((items, 2, depth - 1)),
            dma((items, depth)), dma((items, depth)),
            dma((leaves - 1,)), dma((leaves - 1,)),
            dma((group, 6)), dma((group, 6)),
            dma((group, 6)), dma((group, 6)),
            dma((group, 6)), dma((group, 6)),
            dma((group, 6)), dma((group, 6)),
            dma((2,)), dma((2,)),
            dma((group + 1,)),
        ],
        compiler_params=pltpu.CompilerParams(
            collective_id=0, has_side_effects=True, vmem_limit_bytes=56 * 1024 * 1024
        ),
    )(panel, inv_diag, sigma_root, structure)
    return pl.pallas_call(
        hand_over, out_shape=tuple(jax.ShapeDtypeStruct(one.shape, one.dtype) for one in made)
    )(*made)


def solution(mesh):
    placed = (P("leaf", ("row", "col")), P(), P("leaf", "row", "col"), P("leaf", None, "row"))
    return jax.shard_map(
        body,
        mesh=mesh,
        in_specs=placed,
        out_specs=(P("leaf", "row", "col"), P("leaf", "row", "col")),
        check_vma=False,
    )
```
